128 devices in a mesh: clip: 64 (over y, x, z_hi, core), seq: 2 (over z_lo).
Axes of the slice: x: 4, y: 4, z: 4 (z_hi: 2, z_lo: 2; z = z_hi * 2 + z_lo), core: 2. Of those that a mesh axis runs over, the one named last changes fastest.
Arguments:
- latent_tokens: bfloat16 [64, 256, 1536], P('clip', 'seq'), may hold values from -6 to 6
- time_embed: float32 [64, 6, 1536], P('clip'), may hold values from -4 to 4
- text_tokens: bfloat16 [64, 512, 1536], P('clip', 'seq'), may hold values from -6 to 6
- positions: int32 [64, 3, 256], P('clip', None, 'seq'), may hold values from 0 to 30, as said below
- w_qkv: bfloat16 [1536, 4608], P(('clip', 'seq')), may hold values from -0.15625 to 0.15625
- attn_out: bfloat16 [1536, 1536], P(('clip', 'seq')), may hold values from -1.5 to 1.5
- cross_q: bfloat16 [1536, 1536], P(('clip', 'seq')), may hold values from -0.15625 to 0.15625
- cross_kv: bfloat16 [1536, 3072], P(('clip', 'seq')), may hold values from -0.15625 to 0.15625
- cross_out: bfloat16 [1536, 1536], P(('clip', 'seq')), may hold values from -2 to 2
- mlp_in: bfloat16 [1536, 8960], P(('clip', 'seq')), may hold values from -0.15625 to 0.15625
- mlp_out: bfloat16 [8960, 1536], P(('clip', 'seq')), may hold values from -0.0625 to 0.0625
- gain_q: bfloat16 [1536], P(('clip', 'seq')), may hold values from 0.5 to 1.5
- gain_k: bfloat16 [1536], P(('clip', 'seq')), may hold values from 0.5 to 1.5
- gain_cq: bfloat16 [1536], P(('clip', 'seq')), may hold values from 0.5 to 1.5
- gain_ck: bfloat16 [1536], P(('clip', 'seq')), may hold values from 0.5 to 1.5
- norm_weight: bfloat16 [1536], P(('clip', 'seq')), may hold values from 0.5 to 1.5
- norm_bias: bfloat16 [1536], P(('clip', 'seq')), may hold values from -4 to 4
- modulation: bfloat16 [6, 1536], P(None, ('clip', 'seq')), may hold values from -6 to 6
- cotangent: bfloat16 [64, 256, 1536], P('clip', 'seq'), may hold values from -6 to 6
Outputs:
- block_output: bfloat16 [64, 256, 1536], P('clip', 'seq')
- input_grad: float32 [64, 256, 1536], P('clip', 'seq')
- grad_w_qkv: float32 [1536, 4608], P(('clip', 'seq'))
- grad_attn_out: float32 [1536, 1536], P(('clip', 'seq'))
- grad_cross_q: float32 [1536, 1536], P(('clip', 'seq'))
- grad_cross_kv: float32 [1536, 3072], P(('clip', 'seq'))
- grad_cross_out: float32 [1536, 1536], P(('clip', 'seq'))
- grad_mlp_in: float32 [1536, 8960], P(('clip', 'seq'))
- grad_mlp_out: float32 [8960, 1536], P(('clip', 'seq'))
- grad_gain_q: float32 [1536], P(('clip', 'seq'))
- grad_gain_k: float32 [1536], P(('clip', 'seq'))
- grad_gain_cq: float32 [1536], P(('clip', 'seq'))
- grad_gain_ck: float32 [1536], P(('clip', 'seq'))
- grad_norm_weight: float32 [1536], P(('clip', 'seq'))
- grad_norm_bias: float32 [1536], P(('clip', 'seq'))
- grad_modulation: float32 [6, 1536], P(None, ('clip', 'seq'))
The draws below stay inside these ranges and needn't reach their ends.
Inputs may be any that keep to these rules, and one draw needn't show every extreme that they name: positions[c, 0, t], positions[c, 1, t], positions[c, 2, t] are the frame, row and column of the grid cell of token t of clip c; the tokens of a clip take the 2 x 8 x 16 cells of a grid each once, in an order of that clip's own, and each coordinate is shifted by an offset of clip c from 0 to 15; the first clip's offsets are all 15 and the last clip's all 0.
All inputs are finite; a program needn't handle non-finite values.
Results may differ from the reference program's by a relative error of at most 0.025.
Values may be sent and summed in bfloat16 or wider, within the bound.
No kernel may reach another device: no remote copies, remote signals or barrier semaphores. Data moves between devices by JAX's collectives and lax.ppermute only.
A program may use at most 704 MiB of HBM per device.

```python
import jax
import jax.numpy as jnp
from jax import lax

D = 1536
FF = 8960
HEADS = 12
HEAD_DIM = 128
TEXT = 512
ROWS = 8
COLS = 16
TOKENS_CLIP = 256
CLIPS = 64


def draw_positions(key, part):
    offsets = jax.random.randint(jax.random.fold_in(key, 1), (CLIPS, 3, 1), 0, 16)
    offsets = offsets.at[0].set(15)
    offsets = offsets.at[CLIPS - 1].set(0)
    cell_index = jnp.arange(TOKENS_CLIP, dtype=jnp.int32)
    grid_cells = jnp.stack([cell_index // (ROWS * COLS), cell_index // COLS % ROWS, cell_index % COLS], axis=0)
    clip_keys = jax.random.split(jax.random.fold_in(key, 2), CLIPS)
    orders = jax.vmap(lambda clip_key: jax.random.permutation(clip_key, TOKENS_CLIP))(clip_keys)
    placed = jnp.transpose(grid_cells[:, orders], (1, 0, 2))
    return (placed + offsets).astype(jnp.int32)


def shard_levels(key, dims, cuts, low, high):
    def one(position, blocks):
        heights = jax.random.uniform(jax.random.fold_in(jax.random.fold_in(key, 6), position), (blocks,), jnp.float32, low / len(cuts), high / len(cuts))
        return jnp.repeat(jnp.exp(heights), dims[position] // blocks).reshape((-1,) + (1,) * (len(dims) - position - 1))

    factor_of = one(*cuts[0])
    for cut in cuts[1:]:
        factor_of = factor_of * one(*cut)
    return factor_of


def scatter_about(key, dims, scale, reach, shards=(), kind=jnp.bfloat16):
    values = jax.random.normal(key, dims, jnp.float32) * scale
    if len(shards) > 0:
        values = shard_levels(key, dims, shards, -0.22, 0.18) * values
    return jnp.clip(values, min=-reach, max=reach).astype(kind)


def setup_inputs(seed: int = 0) -> dict:
    key_list = jax.random.split(jax.random.key(seed), 20)
    latent_tokens = scatter_about(key_list[0], (CLIPS, TOKENS_CLIP, D), 1.0, 6.0, ((0, 64), (1, 2)))
    time_embed = scatter_about(key_list[1], (CLIPS, 6, D), 0.3, 4.0, ((0, 64),), jnp.float32)
    text_tokens = scatter_about(key_list[2], (CLIPS, TEXT, D), 1.0, 6.0, ((0, 64), (1, 2)))
    positions = draw_positions(jax.random.fold_in(key_list[19], 71), 0)
    w_qkv = scatter_about(key_list[4], (D, 3 * D), D ** -0.5, 0.15625, ((0, 128),))
    attn_out = scatter_about(key_list[5], (D, D), (max(1, D * 3 // TOKENS_CLIP)) ** -0.5, 1.5, ((0, 128),))
    cross_q = scatter_about(key_list[6], (D, D), D ** -0.5, 0.15625, ((0, 128),))
    cross_kv = scatter_about(key_list[7], (D, 2 * D), D ** -0.5, 0.15625, ((0, 128),))
    cross_out = scatter_about(key_list[8], (D, D), (max(1, D * 3 // TEXT)) ** -0.5, 2.0, ((0, 128),))
    mlp_in = scatter_about(key_list[9], (D, FF), D ** -0.5, 0.15625, ((0, 128),))
    mlp_out = scatter_about(key_list[10], (FF, D), FF ** -0.5, 0.0625, ((0, 128),))
    gain_q = jnp.clip(1.0 + 0.1 * jax.random.normal(key_list[11], (D,), jnp.float32), 0.5, 1.5).astype(jnp.bfloat16)
    gain_k = jnp.clip(1.0 + 0.1 * jax.random.normal(key_list[12], (D,), jnp.float32), 0.5, 1.5).astype(jnp.bfloat16)
    gain_cq = jnp.clip(1.0 + 0.1 * jax.random.normal(key_list[13], (D,), jnp.float32), 0.5, 1.5).astype(jnp.bfloat16)
    gain_ck = jnp.clip(1.0 + 0.1 * jax.random.normal(key_list[14], (D,), jnp.float32), 0.5, 1.5).astype(jnp.bfloat16)
    norm_weight = jnp.clip(1.0 + 0.1 * jax.random.normal(key_list[15], (D,), jnp.float32), 0.5, 1.5).astype(jnp.bfloat16)
    norm_bias = scatter_about(key_list[16], (D,), 0.3, 4.0, ((0, 128),))
    modulation = scatter_about(key_list[17], (6, D), 0.5, 6.0, ((1, 128),))
    cotangent = scatter_about(key_list[18], (CLIPS, TOKENS_CLIP, D), 1.0, 6.0, ((0, 64), (1, 2)))
    return {"latent_tokens": latent_tokens, "time_embed": time_embed, "text_tokens": text_tokens, "positions": positions, "w_qkv": w_qkv, "attn_out": attn_out, "cross_q": cross_q, "cross_kv": cross_kv, "cross_out": cross_out, "mlp_in": mlp_in, "mlp_out": mlp_out, "gain_q": gain_q, "gain_k": gain_k, "gain_cq": gain_cq, "gain_ck": gain_ck, "norm_weight": norm_weight, "norm_bias": norm_bias, "modulation": modulation, "cotangent": cotangent}


@jax.custom_vjp
def low(v):
    return lax.optimization_barrier(v.astype(jnp.bfloat16)).astype(jnp.float32)

@jax.custom_vjp
def low_back(v):
    return v

def low_keep(v):
    return (low(v), None)

def low_pass(kept, grad):
    return (grad,)

def back_keep(v):
    return (v, None)

def back_low(kept, grad):
    return (low(grad),)
low.defvjp(low_keep, low_pass)
low_back.defvjp(back_keep, back_low)
NORM_EPS = 1e-06
HIGHEST = lax.Precision.HIGHEST

def matmul_high(left, right):
    return jnp.dot(left, right, precision=HIGHEST, preferred_element_type=jnp.float32)

def layer_norm(values):
    centred = values - lax.optimization_barrier(jnp.mean(values, axis=-1, keepdims=True))
    return centred * lax.rsqrt(lax.optimization_barrier(jnp.mean(centred * centred, axis=-1, keepdims=True)) + NORM_EPS)

def rms_norm(values, gain_row):
    return values * lax.rsqrt(lax.optimization_barrier(jnp.mean(values * values, axis=-1, keepdims=True)) + NORM_EPS) * gain_row

def inverse_freq(pair_total):
    return 1.0 / 10000.0 ** (jnp.arange(pair_total, dtype=jnp.float32) * 2.0 / (2.0 * pair_total))

def rotary_tables(places_int, head_dim):
    pair_count = head_dim // 2
    side_pairs = pair_count // 3
    frame_pairs = pair_count - 2 * side_pairs
    places = places_int.astype(jnp.float32)
    angles = jnp.concatenate([places[0][:, None] * inverse_freq(frame_pairs)[None, :], places[1][:, None] * inverse_freq(side_pairs)[None, :], places[2][:, None] * inverse_freq(side_pairs)[None, :]], axis=1)
    return (jnp.cos(angles), jnp.sin(angles))

def rotate(values, cos_table, sin_table):
    row_count, head_count, head_width = values.shape
    paired = values.reshape(row_count, head_count, head_width // 2, 2)
    real_part = paired[..., 0]
    imag_part = paired[..., 1]
    cos_rows = cos_table[:, None, :]
    sin_rows = sin_table[:, None, :]
    new_real = real_part * cos_rows - imag_part * sin_rows
    new_imag = real_part * sin_rows + imag_part * cos_rows
    return jnp.stack([new_real, new_imag], axis=-1).reshape(row_count, head_count, head_width)

def attend(query_heads, key_heads, value_heads):
    scores = jnp.einsum('qhd,khd->hqk', query_heads, key_heads, precision=HIGHEST) * HEAD_DIM ** (-0.5)
    scores = low_back(scores)
    weights = low(jax.nn.softmax(scores, axis=-1))
    return jnp.einsum('hqk,khd->qhd', weights, value_heads, precision=HIGHEST)

def block_forward(params, hidden, time_row, text_rows, cos_table, sin_table):
    w_qkv, attn_out, cross_q, cross_kv, cross_out, mlp_in, mlp_out, gain_q, gain_k, gain_cq, gain_ck, norm_weight, norm_bias, modulation = params
    model_width = hidden.shape[1]
    row_count = hidden.shape[0]
    text_count = text_rows.shape[0]
    mod_rows = time_row + modulation
    attn_input = low(layer_norm(hidden) * (1.0 + mod_rows[1]) + mod_rows[0])
    qkv_pre = low_back(matmul_high(attn_input, w_qkv))
    query_rot = rotate(rms_norm(qkv_pre[:, :model_width], gain_q).reshape(row_count, HEADS, HEAD_DIM), cos_table, sin_table)
    key_rot = rotate(rms_norm(qkv_pre[:, model_width:2 * model_width], gain_k).reshape(row_count, HEADS, HEAD_DIM), cos_table, sin_table)
    value_heads = low(qkv_pre[:, 2 * model_width:]).reshape(row_count, HEADS, HEAD_DIM)
    attn_heads = low(low_back(attend(low(query_rot), low(key_rot), value_heads)))
    branch_one = low_back(matmul_high(attn_heads.reshape(row_count, model_width), attn_out))
    after_attn = hidden + branch_one * mod_rows[2]
    cross_input = low(layer_norm(after_attn) * norm_weight + norm_bias)
    cq_pre = low_back(matmul_high(cross_input, cross_q))
    cross_query = low(rms_norm(cq_pre, gain_cq)).reshape(row_count, HEADS, HEAD_DIM)
    ckv_pre = low_back(matmul_high(text_rows, cross_kv))
    cross_key = low(rms_norm(ckv_pre[:, :model_width], gain_ck)).reshape(text_count, HEADS, HEAD_DIM)
    cross_value = low(ckv_pre[:, model_width:]).reshape(text_count, HEADS, HEAD_DIM)
    cross_heads = low(low_back(attend(cross_query, cross_key, cross_value)))
    branch_two = low_back(matmul_high(cross_heads.reshape(row_count, model_width), cross_out))
    after_cross = after_attn + branch_two
    mlp_input = low(layer_norm(after_cross) * (1.0 + mod_rows[4]) + mod_rows[3])
    hidden_pre = low_back(matmul_high(mlp_input, mlp_in))
    activated = low(jax.nn.gelu(hidden_pre, approximate=True))
    branch_three = low_back(matmul_high(activated, mlp_out))
    return after_cross + branch_three * mod_rows[5]

def reference(latent_tokens, time_embed, text_tokens, positions, w_qkv, attn_out, cross_q, cross_kv, cross_out, mlp_in, mlp_out, gain_q, gain_k, gain_cq, gain_ck, norm_weight, norm_bias, modulation, cotangent):
    params = tuple((member.astype(jnp.float32) for member in (w_qkv, attn_out, cross_q, cross_kv, cross_out, mlp_in, mlp_out, gain_q, gain_k, gain_cq, gain_ck, norm_weight, norm_bias, modulation)))

    def per_clip(totals, inputs):
        hidden, time_row, text_rows, places, upstream = inputs
        cos_table, sin_table = rotary_tables(places, HEAD_DIM)

        def forward(param_set, hidden_in):
            return block_forward(param_set, hidden_in, time_row, text_rows, cos_table, sin_table)
        result, pullback = jax.vjp(forward, params, hidden)
        grad_params, grad_hidden = pullback(upstream)
        totals = jax.tree.map(lambda running, change: running + change, totals, grad_params)
        return (totals, (result.astype(jnp.bfloat16), grad_hidden))
    initial = tuple((jnp.zeros(member.shape, jnp.float32) for member in params))
    sequences = (latent_tokens.astype(jnp.float32), time_embed.astype(jnp.float32), text_tokens.astype(jnp.float32), positions, cotangent.astype(jnp.float32))
    totals, (outputs, input_grads) = lax.scan(per_clip, initial, sequences)
    return (outputs, input_grads, totals[0], totals[1], totals[2], totals[3], totals[4], totals[5], totals[6], totals[7], totals[8], totals[9], totals[10], totals[11], totals[12], totals[13])
```

```python
import functools

import jax
import jax.numpy as jnp
from jax import lax
from jax.experimental import pallas as pl
from jax.experimental.pallas import tpu as pltpu
from jax.sharding import Mesh
from jax.sharding import PartitionSpec as P

HEADS = 12
HEAD_DIM = 128
NORM_EPS = 1e-06
SCALE = HEAD_DIM ** (-0.5)

bf16 = jnp.bfloat16
f32 = jnp.float32

GROUP = ("core", "zl")
CHIPS = ("zh", "zl")
LINE = ("zh", "core", "zl")
PLACES = ("y", "x")
SWAP = [(0, 1), (1, 0)]
CROSS = [(0, 3), (3, 0), (1, 2), (2, 1)]


def mm(left, right):
    return jnp.dot(left, right, preferred_element_type=f32)


def mm_tn(left, right):
    return lax.dot_general(left, right, (((0,), (0,)), ((), ())), preferred_element_type=f32)


def mm_nt(left, right):
    return lax.dot_general(left, right, (((1,), (1,)), ((), ())), preferred_element_type=f32)


def swap(array, axis_name):
    return lax.ppermute(array, axis_name, SWAP)


def others(array, axis_name):
    size = lax.axis_size(axis_name)
    return [array] + [
        lax.ppermute(array, axis_name, [(i, i ^ k) for i in range(size)]) for k in range(1, size)
    ]


def in_order(parts, index):
    step = 1
    parts = list(parts)
    while step < len(parts):
        turned = index // step % 2 == 1
        for k in range(len(parts)):
            if k & step == 0:
                low, high = parts[k], parts[k + step]
                parts[k], parts[k + step] = jnp.where(turned, high, low), jnp.where(turned, low, high)
        step *= 2
    return parts


def axis_join(piece, axis_name, dim=0):
    return jnp.concatenate(in_order(others(piece, axis_name), lax.axis_index(axis_name)), dim)


def near_sum(blocks, axis_name):
    size = lax.axis_size(axis_name)
    total = blocks[0].astype(f32)
    for k in range(1, size):
        pairs = [(i, i ^ k) for i in range(size)]
        total = total + lax.ppermute(blocks[k], axis_name, pairs).astype(f32)
    return total


def group_sum(small):
    return (
        small + swap(small, "zl") + swap(small, "core") + lax.ppermute(small, GROUP, CROSS)
    )


def core_sum(small):
    return small + swap(small, "core")


def ordered(mine, other, axis_name, dim):
    first = lax.axis_index(axis_name) == 0
    return jnp.where(
        first, jnp.concatenate([mine, other], dim), jnp.concatenate([other, mine], dim)
    )


def join(piece, axis_name, dim):
    return ordered(piece, swap(piece, axis_name), axis_name, dim)


def halves(whole, axis_name, dim):
    low, high = jnp.split(whole, 2, dim)
    first = lax.axis_index(axis_name) == 0
    return jnp.where(first, low, high), jnp.where(first, high, low)


def trade(whole, axis_name, cut, lay):
    keep, give = halves(whole, axis_name, cut)
    return ordered(keep, swap(give, axis_name), axis_name, lay)


def scatter_sum(partial, axis_name, dim):
    keep, give = halves(partial, axis_name, dim)
    return keep.astype(f32) + swap(give.astype(bf16), axis_name).astype(f32)


def by_seq(rows):
    return rows.reshape(2, rows.shape[0] // 2, rows.shape[1])


def flat(rows):
    return rows.reshape(-1, rows.shape[-1])


def layer_norm(values):
    centred = values - jnp.mean(values, axis=-1, keepdims=True)
    inv = lax.rsqrt(jnp.mean(centred * centred, axis=-1, keepdims=True) + NORM_EPS)
    return centred * inv, inv


def split_norm(values):
    local = values.shape[1]
    mean_here = jnp.mean(values, axis=-1)
    centred = values - mean_here[:, None]
    mine = jnp.stack([mean_here, jnp.sum(centred * centred, axis=-1)])
    other = swap(mine, "core")
    mean = (mine[0] + other[0]) / 2
    apart = mine[0] - mean
    spread = mine[1] + other[1] + 2 * local * apart * apart
    inv = lax.rsqrt(spread / (2 * local) + NORM_EPS)
    return (values - mean[:, None]) * inv[:, None], inv


def turn(values, cos, sin):
    lanes = lax.broadcasted_iota(jnp.int32, values.shape, 1)
    swapped = jnp.where(
        lanes % 2 == 0,
        -pltpu.roll(values, HEAD_DIM - 1, 1),
        pltpu.roll(values, 1, 1),
    )
    return values * cos + swapped * sin


def attend(query, key):
    scores = mm_nt(query, key) * SCALE
    peak = jnp.max(scores, axis=-1, keepdims=True)
    weights = jnp.exp(scores - peak)
    weights = weights / jnp.sum(weights, axis=-1, keepdims=True)
    return weights


def attend_grads(query, key, value, grad):
    weights = attend(query, key)
    grad_weights = mm_nt(grad, value)
    delta = jnp.sum(weights * grad_weights, axis=-1, keepdims=True)
    grad_scores = (weights * (grad_weights - delta)).astype(bf16)
    grad_query = mm(grad_scores, key) * SCALE
    grad_key = mm_tn(grad_scores, query) * SCALE
    grad_value = mm_tn(weights.astype(bf16), grad)
    return grad_query, grad_key, grad_value


def self_forward_kernel(q_ref, k_ref, v_ref, r_ref, gq_ref, gk_ref, cos_ref, sin_ref,
                        qr_ref, kr_ref, vb_ref, o_ref):
    cos, sin = cos_ref[...], sin_ref[...]
    query = turn(q_ref[...] * r_ref[:, 0:1] * gq_ref[...], cos, sin).astype(bf16)
    key = turn(k_ref[...] * r_ref[:, 1:2] * gk_ref[...], cos, sin).astype(bf16)
    value = v_ref[...].astype(bf16)
    qr_ref[...] = query
    kr_ref[...] = key
    vb_ref[...] = value
    weights = attend(query, key).astype(bf16)
    o_ref[...] = mm(weights, value).astype(bf16)


def self_forward(qkv, inverse, gain_q, gain_k, cos, sin, clips):
    rows, local = qkv.shape[0], qkv.shape[1] // 3
    heads, tokens = local // HEAD_DIM, rows // clips

    def at(shift):
        return pl.BlockSpec((tokens, HEAD_DIM), lambda b, h, s=shift: (b, h + s))

    gain = pl.BlockSpec((1, HEAD_DIM), lambda b, h: (0, h))
    table = pl.BlockSpec((tokens, HEAD_DIM), lambda b, h: (b, 0))
    return pl.pallas_call(
        self_forward_kernel,
        grid=(clips, heads),
        in_specs=[at(0), at(heads), at(2 * heads),
                  pl.BlockSpec((tokens, 2), lambda b, h: (b, 0)), gain, gain, table, table],
        out_specs=[at(0)] * 4,
        out_shape=[jax.ShapeDtypeStruct((rows, local), bf16)] * 4,
        cost_estimate=pl.CostEstimate(flops=8 * 10**9, bytes_accessed=10**7, transcendentals=10**6),
        name="self_forward",
    )(qkv, qkv, qkv, inverse, gain_q, gain_k, cos, sin)


def self_backward_kernel(qr_ref, kr_ref, vb_ref, do_ref, q_ref, k_ref, r_ref, gq_ref, gk_ref,
                         cos_ref, sin_ref, uq_ref, uk_ref, dv_ref, part_ref, dgain_ref):
    cos, sin = cos_ref[...], sin_ref[...]
    grad_query, grad_key, grad_value = attend_grads(
        qr_ref[...], kr_ref[...], vb_ref[...], do_ref[...]
    )
    up_q = turn(grad_query, cos, -sin)
    up_k = turn(grad_key, cos, -sin)
    dv_ref[...] = grad_value.astype(bf16)
    vq, vk = up_q * q_ref[...], up_k * k_ref[...]
    dgain_ref[0, 0, 0:1, :] = jnp.sum(vq * r_ref[:, 0:1], axis=0, keepdims=True)
    dgain_ref[0, 0, 1:2, :] = jnp.sum(vk * r_ref[:, 1:2], axis=0, keepdims=True)
    up_q, up_k = up_q * gq_ref[...], up_k * gk_ref[...]
    uq_ref[...] = up_q
    uk_ref[...] = up_k
    mean_q = jnp.sum(vq * gq_ref[...], axis=-1, keepdims=True)
    mean_k = jnp.sum(vk * gk_ref[...], axis=-1, keepdims=True)
    both = jnp.concatenate([mean_q, mean_k], axis=1)

    @pl.when(pl.program_id(1) == 0)
    def _():
        part_ref[...] = both

    @pl.when(pl.program_id(1) > 0)
    def _():
        part_ref[...] += both


def self_backward(qr, kr, vb, grad, qkv, inverse, gain_q, gain_k, cos, sin, clips):
    rows, local = qr.shape
    heads, tokens = local // HEAD_DIM, rows // clips

    def at(shift):
        return pl.BlockSpec((tokens, HEAD_DIM), lambda b, h, s=shift: (b, h + s))

    gain = pl.BlockSpec((1, HEAD_DIM), lambda b, h: (0, h))
    table = pl.BlockSpec((tokens, HEAD_DIM), lambda b, h: (b, 0))
    pair = pl.BlockSpec((tokens, 2), lambda b, h: (b, 0))
    return pl.pallas_call(
        self_backward_kernel,
        grid=(clips, heads),
        in_specs=[at(0)] * 4 + [at(0), at(heads), pair, gain, gain, table, table],
        out_specs=[at(0)] * 3 + [pair, pl.BlockSpec((1, 1, 2, HEAD_DIM), lambda b, h: (b, h, 0, 0))],
        out_shape=[
            jax.ShapeDtypeStruct((rows, local), f32),
            jax.ShapeDtypeStruct((rows, local), f32),
            jax.ShapeDtypeStruct((rows, local), bf16),
            jax.ShapeDtypeStruct((rows, 2), f32),
            jax.ShapeDtypeStruct((clips, heads, 2, HEAD_DIM), f32),
        ],
        cost_estimate=pl.CostEstimate(flops=11 * 10**9, bytes_accessed=10**7, transcendentals=10**6),
        name="self_backward",
    )(qr, kr, vb, grad, qkv, qkv, inverse, gain_q, gain_k, cos, sin)


def cross_forward_kernel(q_ref, r_ref, g_ref, k_ref, v_ref, qn_ref, o_ref):
    tokens, words = q_ref.shape[0] // 2, k_ref.shape[0] // 2
    for clip in range(2):
        rows, text = pl.ds(clip * tokens, tokens), pl.ds(clip * words, words)
        query = (q_ref[rows, :] * r_ref[rows, :] * g_ref[...]).astype(bf16)
        qn_ref[rows, :] = query
        weights = attend(query, k_ref[text, :]).astype(bf16)
        o_ref[rows, :] = mm(weights, v_ref[text, :]).astype(bf16)


def cross_forward(cq, inverse, gain, key, value):
    rows, local = cq.shape
    at = pl.BlockSpec((rows, HEAD_DIM), lambda h: (0, h))
    text = pl.BlockSpec((key.shape[0], HEAD_DIM), lambda h: (0, h))
    return pl.pallas_call(
        cross_forward_kernel,
        grid=(local // HEAD_DIM,),
        in_specs=[at, pl.BlockSpec((rows, 1), lambda h: (0, 0)),
                  pl.BlockSpec((1, HEAD_DIM), lambda h: (0, h)), text, text],
        out_specs=[at, at],
        out_shape=[jax.ShapeDtypeStruct((rows, local), bf16)] * 2,
        cost_estimate=pl.CostEstimate(flops=9 * 10**9, bytes_accessed=10**7, transcendentals=10**6),
        name="cross_forward",
    )(cq, inverse, gain, key, value)


def cross_backward_kernel(qn_ref, k_ref, v_ref, do_ref, dq_ref, dk_ref, dv_ref):
    tokens, words = qn_ref.shape[0] // 2, k_ref.shape[0] // 2
    for clip in range(2):
        rows, text = pl.ds(clip * tokens, tokens), pl.ds(clip * words, words)
        grad_query, grad_key, grad_value = attend_grads(
            qn_ref[rows, :], k_ref[text, :], v_ref[text, :], do_ref[rows, :]
        )
        dq_ref[rows, :] = grad_query
        dk_ref[text, :] = grad_key
        dv_ref[text, :] = grad_value.astype(bf16)


def cross_backward(query, key, value, grad):
    rows, local = query.shape
    at = pl.BlockSpec((rows, HEAD_DIM), lambda h: (0, h))
    text = pl.BlockSpec((key.shape[0], HEAD_DIM), lambda h: (0, h))
    return pl.pallas_call(
        cross_backward_kernel,
        grid=(local // HEAD_DIM,),
        in_specs=[at, text, text, at],
        out_specs=[at, text, text],
        out_shape=[
            jax.ShapeDtypeStruct((rows, local), f32),
            jax.ShapeDtypeStruct(key.shape, f32),
            jax.ShapeDtypeStruct(key.shape, bf16),
        ],
        cost_estimate=pl.CostEstimate(flops=11 * 10**9, bytes_accessed=10**7, transcendentals=10**6),
        name="cross_backward",
    )(query, key, value, grad)


PACK = 256
REST = 768
GELU_A = 0.7978845608028654
GELU_B = 0.044715


def mlp_kernel(core_ref, x_ref, xo_ref, g_ref, go_ref, pack_ref, act_ref, gh_ref, gx_ref, gxo_ref,
               up, down, act, gh, total, total_other, sems, out_sems):
    peers, up_rows, hidden = up.shape
    down_rows, width = down.shape[1:]
    half = width // 2
    cuts = [0, hidden // PACK // 2 * PACK, hidden]
    loads, last = [], 0
    for k in range(2):
        first, last = last, -(-cuts[k + 1] // down_rows)
        moves = [
            (pack_ref.at[:, pl.ds(at // PACK * up_rows, up_rows), :], up.at[:, :, pl.ds(at, PACK)])
            for at in range(cuts[k], cuts[k + 1], PACK)
        ]
        for at in range(0, width, PACK):
            line = hidden // PACK * up_rows + at // PACK * down_rows
            moves.append(
                (
                    pack_ref.at[pl.ds(first, last - first), pl.ds(line, down_rows), :],
                    down.at[pl.ds(first, last - first), :, pl.ds(at, PACK)],
                )
            )
        loads.append([pltpu.make_async_copy(*m, sems.at[k, i]) for i, m in enumerate(moves)])
        for copy in loads[-1]:
            copy.start()
    down_flat = down.reshape(peers * down_rows, width)
    up_flat = up.reshape(peers * up_rows, hidden)
    mine = pl.ds(pl.multiple_of(core_ref[0] * half, half), half)
    other = pl.ds(pl.multiple_of((1 - core_ref[0]) * half, half), half)
    stores = []
    for k in range(2):
        for copy in loads[k]:
            copy.wait()
        cols = pl.ds(cuts[k], cuts[k + 1] - cuts[k])
        pre = mm(x_ref[...], up_flat[mine, cols]) + mm(xo_ref[...], up_flat[other, cols])
        grad = mm_nt(g_ref[...], down_flat[cols, mine]) + mm_nt(go_ref[...], down_flat[cols, other])
        square = pre * pre
        tanh = jnp.tanh(GELU_A * pre * (1.0 + GELU_B * square))
        share = 0.5 * (1.0 + tanh)
        act[:, cols] = (pre * share).astype(bf16)
        slope = share + pre * (0.5 * GELU_A) * (1.0 - tanh * tanh) * (1.0 + 3 * GELU_B * square)
        grad = (grad * slope).astype(bf16)
        gh[:, cols] = grad
        for i, (here, there) in enumerate(((act, act_ref), (gh, gh_ref))):
            stores.append(pltpu.make_async_copy(here.at[:, cols], there.at[:, cols], out_sems.at[k, i]))
            stores[-1].start()
        for rows, sums, out in ((mine, total, gx_ref), (other, total_other, gxo_ref)):
            part = mm_nt(grad, up_flat[rows, cols])
            if k == 0:
                sums[...] = part
            else:
                out[...] = (sums[...] + part).astype(bf16)
    for copy in stores:
        copy.wait()


def mlp(core, inputs, grads, packed, up_rows, hidden, down_rows):
    rows, half = inputs[0].shape
    width = 2 * half
    peers = packed.shape[0]
    copies = -(-hidden // PACK // 2) + width // PACK
    vmem = pl.BlockSpec(memory_space=pltpu.VMEM)
    any_space = pl.BlockSpec(memory_space=pl.ANY)
    return pl.pallas_call(
        mlp_kernel,
        in_specs=[pl.BlockSpec(memory_space=pltpu.SMEM)] + [vmem] * 4 + [any_space],
        out_specs=[any_space, any_space, vmem, vmem],
        out_shape=[
            jax.ShapeDtypeStruct((rows, hidden), bf16),
            jax.ShapeDtypeStruct((rows, hidden), bf16),
            jax.ShapeDtypeStruct((rows, half), bf16),
            jax.ShapeDtypeStruct((rows, half), bf16),
        ],
        scratch_shapes=[
            pltpu.VMEM((peers, up_rows, hidden), bf16),
            pltpu.VMEM((peers, down_rows, width), bf16),
            pltpu.VMEM((rows, hidden), bf16),
            pltpu.VMEM((rows, hidden), bf16),
            pltpu.VMEM((rows, half), f32),
            pltpu.VMEM((rows, half), f32),
            pltpu.SemaphoreType.DMA((2, copies)),
            pltpu.SemaphoreType.DMA((2, 2)),
        ],
        compiler_params=pltpu.CompilerParams(vmem_limit_bytes=56 * 2**20),
        cost_estimate=pl.CostEstimate(
            flops=6 * rows * width * hidden, bytes_accessed=packed.size * 2, transcendentals=rows * hidden
        ),
        name="mlp",
    )(core, *inputs, *grads, packed)


def tn_pack_kernel(place, x_ref, g_ref, *rest):
    pack_ref, held, sems = rest[-3:]
    peers, rows, _ = held.shape[1:]
    slots = held.shape[0]
    copies = []
    for k in range(slots):
        grad = g_ref[:, k * REST : (k + 1) * REST]
        lines = held.at[k].reshape(peers * rows, REST)
        lines[...] = mm_tn(x_ref[...], grad).astype(bf16)
        copies.append(
            pltpu.make_async_copy(
                held.at[k], pack_ref.at[:, pl.ds((place + k) * rows, rows), :], sems.at[k]
            )
        )
        copies[-1].start()
    for copy in copies:
        copy.wait()


def tn_pack(left, right, place, places, peers, packed=None):
    width, slots = left.shape[1], right.shape[1] // REST
    rows = width // peers
    vmem = pl.BlockSpec(memory_space=pltpu.VMEM)
    any_space = pl.BlockSpec(memory_space=pl.ANY)
    given = [] if packed is None else [packed]
    return pl.pallas_call(
        functools.partial(tn_pack_kernel, place),
        in_specs=[vmem, vmem] + [any_space] * len(given),
        out_specs=any_space,
        out_shape=jax.ShapeDtypeStruct((peers, places * rows, REST), bf16),
        scratch_shapes=[pltpu.VMEM((slots, peers, rows, REST), bf16), pltpu.SemaphoreType.DMA((slots,))],
        input_output_aliases={2: 0} if given else {},
        compiler_params=pltpu.CompilerParams(vmem_limit_bytes=56 * 2**20),
        cost_estimate=pl.CostEstimate(
            flops=2 * left.size * right.shape[1], bytes_accessed=2 * width * right.shape[1], transcendentals=0
        ),
        name="tn_pack",
    )(left, right, *given)


def mlp_grads_kernel(core_ref, x_ref, xo_ref, gh_ref, act_ref, g_ref, go_ref, pack_ref, up, down, up_sems, down_sems):
    copies = []
    blocks, peers, rows, _ = up.shape
    some = peers // 2
    line = blocks * rows
    for part, left in enumerate((x_ref, xo_ref)):
        first = core_ref[0] if part == 0 else 1 - core_ref[0]
        grad = mm_tn(left[...], gh_ref[...]).astype(bf16)
        for k in range(blocks):
            held = up.at[k, pl.ds(part * some, some)]
            held[...] = grad[:, k * PACK : (k + 1) * PACK].reshape(some, rows, PACK)
            there = pack_ref.at[pl.ds(first * some, some), pl.ds(k * rows, rows), :]
            copies.append(pltpu.make_async_copy(held, there, up_sems.at[part, k]))
            copies[-1].start()
    blocks, _, rows, _ = down.shape
    for part, right in enumerate((g_ref, go_ref)):
        first = core_ref[0] if part == 0 else 1 - core_ref[0]
        grad = mm_tn(act_ref[...], right[...]).astype(bf16)
        for k in range(blocks // 2):
            held = down.at[part * (blocks // 2) + k]
            held[...] = grad[:, k * PACK : (k + 1) * PACK].reshape(peers, rows, PACK)
            at = pl.multiple_of(line + (first * (blocks // 2) + k) * rows, 16)
            there = pack_ref.at[:, pl.ds(at, rows), :]
            copies.append(pltpu.make_async_copy(held, there, down_sems.at[part, k]))
            copies[-1].start()
    for copy in copies:
        copy.wait()


def mlp_grads(core, inputs, grad_hidden, activated, grads, peers):
    width, hidden = 2 * inputs[0].shape[1], activated.shape[1]
    up_rows, down_rows = width // peers, hidden // peers
    lines = hidden // PACK * up_rows + width // PACK * down_rows
    vmem = pl.BlockSpec(memory_space=pltpu.VMEM)
    return pl.pallas_call(
        mlp_grads_kernel,
        in_specs=[pl.BlockSpec(memory_space=pltpu.SMEM)] + [vmem] * 6,
        out_specs=pl.BlockSpec(memory_space=pl.ANY),
        out_shape=jax.ShapeDtypeStruct((peers, lines, PACK), bf16),
        scratch_shapes=[
            pltpu.VMEM((hidden // PACK, peers, up_rows, PACK), bf16),
            pltpu.VMEM((width // PACK, peers, down_rows, PACK), bf16),
            pltpu.SemaphoreType.DMA((2, hidden // PACK)),
            pltpu.SemaphoreType.DMA((2, width // PACK // 2)),
        ],
        compiler_params=pltpu.CompilerParams(vmem_limit_bytes=56 * 2**20),
        cost_estimate=pl.CostEstimate(
            flops=4 * width * inputs[0].shape[0] * hidden, bytes_accessed=4 * width * hidden, transcendentals=0
        ),
        name="mlp_grads",
    )(core, *inputs, grad_hidden, activated, *grads)


def tail_kernel(core_ref, x_ref, g_ref, w_ref, n_ref, small_ref, lines_ref, keep_ref, give_ref):
    cols, some = g_ref.shape[1], x_ref.shape[0] // 2
    ones = jnp.ones((x_ref.shape[0], 128), bf16)
    part = mm_nt(g_ref[...], w_ref[...])
    low = part.astype(bf16)
    first = mm_tn(low, ones)
    second = mm_tn((part * n_ref[...].astype(f32)).astype(bf16), ones)
    lane = lax.broadcasted_iota(jnp.int32, first.shape, 1)
    small = jnp.where(lane == 6, first, jnp.where(lane == 7, second, small_ref[...]))
    lines_ref[:, cols:] = small.astype(bf16)
    zero = core_ref[0] == 0
    keep_ref[...] = jnp.where(zero, low[:some], low[some:])
    give_ref[...] = jnp.where(zero, low[some:], low[:some])
    half = x_ref.shape[1] // 2
    for k in range(2):
        rows = pl.ds(k * half, half)
        lines_ref[rows, :cols] = mm_tn(x_ref[:, rows], g_ref[...]).astype(bf16)


def tail(core, inputs, grad, weight, norm, small):
    rows, width = inputs.shape
    out = [
        jax.ShapeDtypeStruct((width, grad.shape[1] + 128), bf16),
        jax.ShapeDtypeStruct((rows // 2, width), bf16),
        jax.ShapeDtypeStruct((rows // 2, width), bf16),
    ]
    vmem = pl.BlockSpec(memory_space=pltpu.VMEM)
    return pl.pallas_call(
        tail_kernel,
        in_specs=[pl.BlockSpec(memory_space=pltpu.SMEM)] + [vmem] * 5,
        out_specs=[vmem] * 3,
        out_shape=out,
        compiler_params=pltpu.CompilerParams(vmem_limit_bytes=56 * 2**20),
        cost_estimate=pl.CostEstimate(flops=8 * 10**9, bytes_accessed=10**7, transcendentals=0),
        name="tail",
    )(core, inputs, grad, weight, norm, small)


def inverse_freq(pair_total):
    return 1.0 / 10000.0 ** (jnp.arange(pair_total, dtype=f32) * 2.0 / (2.0 * pair_total))


def rotary_tables(places):
    pair_count = HEAD_DIM // 2
    side = pair_count // 3
    frame = pair_count - 2 * side
    freq = jnp.concatenate([inverse_freq(frame), inverse_freq(side), inverse_freq(side)])
    freq = jnp.repeat(freq, 2)[None, :]
    pair = lax.broadcasted_iota(jnp.int32, (1, HEAD_DIM), 1) // 2
    angles = jnp.where(
        pair < frame,
        places[0][:, None],
        jnp.where(pair < frame + side, places[1][:, None], places[2][:, None]),
    ) * freq
    return jnp.cos(angles), jnp.sin(angles)


def columns_for(weight, count, owners):
    rows = weight.shape[0]
    parts = jnp.transpose(weight.reshape(rows, count, owners, -1), (2, 0, 1, 3))
    return parts.reshape(owners, rows, -1)


def along_line(parts):
    return lax.all_to_all(parts, LINE, split_axis=0, concat_axis=0, tiled=True)


def for_line(group_parts=None, core_parts=None):
    if core_parts is not None:
        group_parts = jnp.repeat(core_parts, 2, axis=0)
    return jnp.concatenate([group_parts, group_parts], 0)


def first_then(first, *then):
    return lax.optimization_barrier((first, *then))[1:]


def on_device(
    latent_tokens, time_embed, text_tokens, positions,
    w_qkv, attn_out, cross_q, cross_kv, cross_out, mlp_in, mlp_out,
    gain_q, gain_k, gain_cq, gain_ck, norm_weight, norm_bias, modulation, cotangent,
):
    peers = lax.axis_size(PLACES)
    core, zl = lax.axis_index("core"), lax.axis_index("zl")
    width = latent_tokens.shape[2]
    half, local = width // 2, width // 4
    clips = 2
    rows_each = w_qkv.shape[0]
    line_rows = 8 * rows_each
    hid_each = mlp_out.shape[0]
    hid_pad = -(-hid_each * peers // 256) * 256 // peers
    hidden = peers * hid_pad

    x_mine = latent_tokens[0]
    x_wide = join(join(x_mine, "zl", 0), "core", 0)
    text = join(join(text_tokens[0], "zl", 0), "core", 0)
    small = jnp.concatenate(
        [v[None] for v in (gain_q, gain_k, gain_cq, gain_ck, norm_weight, norm_bias)] + [modulation], 0
    )
    small = jnp.pad(small.T, ((0, 0), (0, 116)))
    shard = along_line(
        jnp.concatenate(
            [
                for_line(group_parts=columns_for(w_qkv, 3, 4)),
                for_line(core_parts=columns_for(attn_out, 1, 2)),
                jnp.broadcast_to(small, (8, *small.shape)),
            ],
            axis=2,
        )
    ).reshape(line_rows, -1)
    first_weight = lax.all_gather(shard[:, : 3 * local + half], PLACES, axis=0, tiled=True)
    qkv_weight, out_weight = first_weight[:, : 3 * local], first_weight[:, 3 * local :]
    whole = shard[:, 3 * local + half : 3 * local + half + 12].T.reshape(1, -1)
    whole = axis_join(axis_join(whole, "x"), "y").reshape(peers, 12, line_rows)
    whole = jnp.transpose(whole, (1, 0, 2)).reshape(12, width).astype(f32)

    parts = jnp.concatenate(
        [columns_for(cross_q, 1, 2), columns_for(cross_kv, 2, 2), columns_for(cross_out, 1, 2)], axis=2
    )
    whole, parts = lax.optimization_barrier((whole, parts))
    cross_shard = along_line(for_line(core_parts=parts)).reshape(line_rows, -1)
    cross_weight = lax.all_gather(cross_shard, PLACES, axis=0, tiled=True)
    cq_weight = cross_weight[:, :half]
    ckv_weight = cross_weight[:, half : 3 * half]
    co_weight = cross_weight[:, 3 * half :]

    time_rows = join(time_embed, "core", 0)
    mod_wide = time_rows + whole[None, 6:]
    mod_mine = time_embed[0] + whole[6:]

    def here(rows, cut):
        picked = jnp.split(rows, 2, -1)
        rows = jnp.where(core == 0, picked[0], picked[1])
        if cut == 4:
            picked = jnp.split(rows, 2, -1)
            rows = jnp.where(zl == 0, picked[0], picked[1])
        return rows

    mod = here(mod_wide, 2)
    g_q, g_k = here(whole[0:1], 4), here(whole[1:2], 4)
    g_cq, g_ck, n_w, n_b = (here(whole[i : i + 1], 2) for i in range(2, 6))
    tokens = latent_tokens.shape[1]

    def per_clip(row):
        rows = mod[:, row]
        return jnp.broadcast_to(rows[:, None], (clips, tokens, half)).reshape(-1, half)

    places = join(join(positions[0].astype(f32), "zl", 1), "core", 1)
    cos, sin = rotary_tables(places)
    x_here = trade(x_mine, "core", 1, 0).astype(f32)
    up_here = trade(cotangent[0], "core", 1, 0).astype(f32)
    norm_wide, _ = layer_norm(x_wide.astype(f32))
    attn_input = norm_wide.reshape(clips, -1, width) * (1.0 + mod_wide[:, 1:2]) + mod_wide[:, 0:1]
    attn_input = flat(attn_input).astype(bf16)
    attn_input, text, x_here, up_here = lax.optimization_barrier((attn_input, text, x_here, up_here))

    qkv = mm(attn_input, qkv_weight)
    squares = jnp.sum((qkv * qkv).reshape(-1, 3, local)[:, :2], axis=-1).T
    inv_qk = lax.rsqrt(group_sum(squares) / width + NORM_EPS).T
    qr, kr, vb, heads = self_forward(qkv, inv_qk, g_q, g_k, cos, sin, clips)
    heads = flat(trade(heads.reshape(2, -1, local), "zl", 1, 2))
    attn_tokens = join(heads, "core", 1)

    up = mlp_in.reshape(rows_each, peers, 8, hid_each)
    up = jnp.pad(up, ((0, 0), (0, 0), (0, 0), (0, hid_pad - hid_each)))
    up = jnp.transpose(up, (2, 0, 1, 3)).reshape(8, rows_each, hidden)
    attn_tokens, up = lax.optimization_barrier((attn_tokens, up))
    up_shard = along_line(up).reshape(line_rows, hidden)
    down = jnp.pad(mlp_out, ((0, hid_pad - hid_each), (0, 0)))
    mlp_shard = jnp.concatenate(
        [up_shard[:, at : at + PACK] for at in range(0, hidden, PACK)]
        + [down[:, at : at + PACK] for at in range(0, width, PACK)],
        axis=0,
    )
    mlp_pack = lax.all_gather(mlp_shard, PLACES, axis=0)

    branch_one = mm(attn_tokens, out_weight)
    after_attn = x_here + branch_one * per_clip(2)
    norm_two, inv_two = split_norm(after_attn)
    cross_input = join((norm_two * n_w + n_b).astype(bf16), "core", 1)
    grad_three = (up_here * per_clip(5)).astype(bf16)
    cross_input, grad_three = lax.optimization_barrier((cross_input, grad_three))
    grad_three = others(grad_three, CHIPS)

    ckv = mm(text, ckv_weight)
    ck_pre = ckv[:, :half]
    inv_ck = lax.rsqrt(core_sum(jnp.sum(ck_pre * ck_pre, axis=-1)[None]) / width + NORM_EPS)[0]
    cross_key = (ck_pre * inv_ck[:, None] * g_ck).astype(bf16)
    cross_value = ckv[:, half:].astype(bf16)
    cq_pre = mm(cross_input, cq_weight)
    cq_pre, *grad_three = lax.optimization_barrier((cq_pre, *grad_three))

    def both_cores(pieces):
        lines = jnp.concatenate(pieces, 0)
        return lines, swap(lines, "core")

    grad_three = both_cores(grad_three)
    inv_cq = lax.rsqrt(core_sum(jnp.sum(cq_pre * cq_pre, axis=-1)[None]) / width + NORM_EPS)[0]
    cross_query, cross_heads = cross_forward(cq_pre, inv_cq[:, None], g_cq, cross_key, cross_value)
    cross_tokens = join(cross_heads, "core", 1)
    after_cross = after_attn + mm(cross_tokens, co_weight)

    norm_three, inv_three = split_norm(after_cross)
    mlp_input = (norm_three * (1.0 + per_clip(4)) + per_clip(3)).astype(bf16)
    mlp_input = both_cores(others(mlp_input, CHIPS))
    core_row = jnp.full((1,), core, jnp.int32)
    activated, grad_hidden, keep, give = mlp(
        core_row, mlp_input, grad_three, mlp_pack, line_rows, hidden, hid_pad
    )

    def core_lines(keep, give):
        lines = keep.astype(f32) + swap(give, "core").astype(f32)
        return lines[: 2 * tokens], jnp.split(lines[2 * tokens :].astype(bf16), 3, 0)

    near, far = core_lines(keep, give)
    grad_mlp_input = near_sum([near, *far], CHIPS)
    down_weight = jnp.concatenate(
        [
            mlp_pack[:, at : at + hid_pad].reshape(hidden, PACK)
            for at in range(line_rows * (hidden // PACK), mlp_pack.shape[1], hid_pad)
        ],
        axis=1,
    )
    near, far = core_lines(*halves(mm(activated, down_weight).astype(bf16), "core", 1))
    mlp_lines = mlp_grads(core_row, mlp_input, grad_hidden, activated, grad_three, peers)
    mlp_lines = mlp_lines.reshape(-1, PACK)
    mlp_sum = lax.psum_scatter(mlp_lines, PLACES, scatter_dimension=0, tiled=True)

    def norm_back(grad, scaled, norm, inv):
        sums = core_sum(jnp.stack([jnp.sum(scaled, axis=-1), jnp.sum(scaled * norm, axis=-1)])) / width
        return (scaled - sums[0][:, None] - norm * sums[1][:, None]) * inv[:, None]

    grad_mod3 = jnp.sum(grad_mlp_input, axis=0)
    grad_mod4 = jnp.sum(grad_mlp_input * norm_three, axis=0)
    grad_cross = up_here + norm_back(
        grad_mlp_input, grad_mlp_input * (1.0 + per_clip(4)), norm_three, inv_three
    )
    grad_two = grad_cross.astype(bf16)

    grad_heads = scatter_sum(mm_nt(grad_two, co_weight).astype(bf16), "core", 1).astype(bf16)
    rest_lines = tn_pack(cross_tokens, grad_two, 4, 5, peers)
    grad_heads, near, *far = lax.optimization_barrier((grad_heads, near, *far))
    far = [lax.ppermute(far[k], CHIPS, [(i, i ^ (k + 1)) for i in range(4)]) for k in range(3)]
    up_cq, up_ck, up_cv = cross_backward(cross_query, cross_key, cross_value, grad_heads)
    up_cq, *far = lax.optimization_barrier((up_cq, *far))
    branch_three = near + sum(part.astype(f32) for part in far)
    result_here = (after_cross + branch_three * per_clip(5)).astype(bf16)
    grad_mod5 = jnp.sum(up_here * branch_three, axis=0)
    result = trade(result_here, "core", 0, 1)

    def rms_back(grad, pre, inv, gain):
        mean = core_sum(jnp.sum(grad * pre * gain, axis=-1)[None])[0] / width
        gain_grad = jnp.sum(grad * pre * inv[:, None], axis=0)
        return (grad * gain - pre * (inv * inv * mean)[:, None]) * inv[:, None], gain_grad

    grad_cq, grad_gain_cq = rms_back(up_cq, cq_pre, inv_cq, g_cq)
    grad_cq = grad_cq.astype(bf16)
    grad_cross_input = scatter_sum(mm_nt(grad_cq, cq_weight).astype(bf16), "core", 1)
    grad_ck, grad_gain_ck = rms_back(up_ck, ck_pre, inv_ck, g_ck)
    grad_ckv = jnp.concatenate([grad_ck.astype(bf16), up_cv], axis=1)
    rest_lines = tn_pack(cross_input, grad_cq, 1, 5, peers, rest_lines)
    rest_lines = tn_pack(text, grad_ckv, 2, 5, peers, rest_lines)
    grad_n_w = jnp.sum(grad_cross_input * norm_two, axis=0)
    grad_n_b = jnp.sum(grad_cross_input, axis=0)
    grad_attn = grad_cross + norm_back(grad_cross_input, grad_cross_input * n_w, norm_two, inv_two)
    grad_attn_mine = trade(grad_attn, "core", 0, 1)

    grad_one = (grad_attn * per_clip(2)).astype(bf16)
    grad_mod2 = jnp.sum(grad_attn * branch_one, axis=0)
    grad_heads = scatter_sum(mm_nt(grad_one, out_weight).astype(bf16), "core", 1).astype(bf16)
    grad_heads = flat(trade(by_seq(grad_heads), "zl", 2, 1))
    rest_lines = tn_pack(attn_tokens, grad_one, 0, 5, peers, rest_lines)
    mlp_sum, rest_lines = lax.optimization_barrier((mlp_sum, rest_lines))
    rest_sum = lax.psum_scatter(rest_lines.reshape(-1, REST), PLACES, scatter_dimension=0, tiled=True)
    up_q, up_k, grad_v, part, dgain = self_backward(
        qr, kr, vb, grad_heads, qkv, inv_qk, g_q, g_k, cos, sin, clips
    )
    mean_qk = group_sum(part.T) / width
    pull = (mean_qk * (inv_qk * inv_qk).T).T
    grad_q = (up_q - qkv[:, :local] * pull[:, 0:1]) * inv_qk[:, 0:1]
    grad_k = (up_k - qkv[:, local : 2 * local] * pull[:, 1:2]) * inv_qk[:, 1:2]
    grad_qkv = jnp.concatenate([grad_q.astype(bf16), grad_k.astype(bf16), grad_v], axis=1)
    dgain = jnp.transpose(jnp.sum(dgain, axis=0), (1, 0, 2)).reshape(2, local)

    dgain = jnp.where(zl == 0, jnp.pad(dgain, ((0, 0), (0, local))), jnp.pad(dgain, ((0, 0), (local, 0))))
    halfs = jnp.concatenate(
        [
            dgain,
            jnp.stack(
                [
                    grad_gain_cq, grad_gain_ck, grad_n_w, grad_n_b,
                    jnp.zeros_like(grad_n_b), jnp.zeros_like(grad_n_b),
                    grad_mod2, grad_mod3, grad_mod4, grad_mod5,
                ]
            ),
        ],
        0,
    )
    smalls = jnp.where(
        core == 0, jnp.pad(halfs, ((0, 0), (0, half))), jnp.pad(halfs, ((0, 0), (half, 0)))
    )
    small_cols = jnp.pad(smalls.T, ((0, 0), (0, 116)))
    last_lines, keep, give = tail(
        core_row, attn_input, grad_qkv, qkv_weight, norm_wide.astype(bf16), small_cols
    )
    last_parts = lax.all_to_all(
        last_lines.reshape(peers, line_rows, -1), PLACES, split_axis=0, concat_axis=0, tiled=True
    )

    grad_attn_input = keep.astype(f32) + swap(give, "core").astype(f32)
    grad_attn_input = scatter_sum(grad_attn_input, "zl", 0)
    norm_one, inv_one = layer_norm(x_mine.astype(f32))
    scaled = grad_attn_input * (1.0 + mod_mine[1:2])
    input_grad = grad_attn_mine + inv_one * (
        scaled
        - jnp.mean(scaled, axis=-1, keepdims=True)
        - norm_one * jnp.mean(scaled * norm_one, axis=-1, keepdims=True)
    )
    mlp_sum, input_grad, last_parts, rest_sum = lax.optimization_barrier(
        (mlp_sum, input_grad, last_parts, rest_sum)
    )
    up_lines = line_rows * (hidden // PACK)
    last_sum = jnp.sum(last_parts.astype(f32), axis=0).astype(bf16)
    rest = jnp.concatenate(
        jnp.split(rest_sum, 5, 0) + [last_sum] + jnp.split(mlp_sum[:up_lines], hidden // PACK, 0), axis=1
    )
    lines = along_line(rest.reshape(8, rows_each, -1))
    up_rows = lines[..., -hidden:].reshape(8, rows_each, peers, hid_pad)[..., :hid_each]
    grad_mlp_in = jnp.transpose(up_rows, (1, 2, 0, 3)).reshape(rows_each, -1).astype(f32)
    down_rows = jnp.concatenate(jnp.split(mlp_sum[up_lines:], width // PACK, 0), axis=1)
    grad_mlp_out = down_rows[:hid_each].astype(f32)
    lines = lines[..., :-hidden].astype(f32).reshape(2, 2, 2, rows_each, -1)
    sides = lines[0, :, 0] + lines[0, :, 1] + lines[1, :, 0] + lines[1, :, 1]
    qkv_lines = (lines[0] + lines[1]).reshape(4, rows_each, -1)[..., 5 * REST : 5 * REST + 3 * local]
    grad_qkv_rows = jnp.transpose(qkv_lines.reshape(4, rows_each, 3, local), (1, 2, 0, 3))
    grad_qkv_rows = grad_qkv_rows.reshape(rows_each, -1)
    small_sum = (sides[0] + sides[1])[:, 5 * REST + 3 * local : 5 * REST + 3 * local + 12].T

    def whole_of(first, count):
        return jnp.concatenate(
            [
                sides[side, :, at * REST : (at + 1) * REST]
                for at in range(first, first + count)
                for side in range(2)
            ],
            axis=1,
        )

    return (
        result[None],
        input_grad[None],
        grad_qkv_rows, whole_of(0, 1), whole_of(1, 1), whole_of(2, 2), whole_of(4, 1),
        grad_mlp_in, grad_mlp_out,
        small_sum[0], small_sum[1], small_sum[2], small_sum[3], small_sum[4], small_sum[5],
        small_sum[6:],
    )


def solution(mesh):
    places = mesh.devices.size // 8
    across = min(places, 4)
    lines = Mesh(
        mesh.devices.reshape(places // across, across, 2, 2, 2), ("y", "x", "zh", "core", "zl")
    )
    clip = ("y", "x", "zh", "core")
    every = (*clip, "zl")
    tokens = P(clip, "zl", None)
    rows = P(every, None)
    return jax.shard_map(
        on_device,
        mesh=lines,
        in_specs=(tokens, P(clip, None, None), tokens, P(clip, None, "zl"))
        + (rows,) * 7 + (P(every),) * 6 + (P(None, every), tokens),
        out_specs=(tokens, tokens) + (rows,) * 7 + (P(every),) * 6 + (P(None, every),),
        check_vma=False,
    )
```

```python
import functools

import jax
import jax.numpy as jnp
from jax import lax
from jax.experimental import pallas as pl
from jax.experimental.pallas import tpu as pltpu
from jax.sharding import Mesh
from jax.sharding import PartitionSpec as P

HEADS = 12
HEAD_DIM = 128
NORM_EPS = 1e-06
SCALE = HEAD_DIM ** (-0.5)

bf16 = jnp.bfloat16
f32 = jnp.float32

GROUP = ("core", "zl")
CHIPS = ("zh", "zl")
LINE = ("zh", "core", "zl")
PLACES = ("y", "x")
SWAP = [(0, 1), (1, 0)]
CROSS = [(0, 3), (3, 0), (1, 2), (2, 1)]


def mm(left, right):
    return jnp.dot(left, right, preferred_element_type=f32)


def mm_tn(left, right):
    return lax.dot_general(left, right, (((0,), (0,)), ((), ())), preferred_element_type=f32)


def mm_nt(left, right):
    return lax.dot_general(left, right, (((1,), (1,)), ((), ())), preferred_element_type=f32)


def swap(array, axis_name):
    return lax.ppermute(array, axis_name, SWAP)


def others(array, axis_name):
    size = lax.axis_size(axis_name)
    return [array] + [
        lax.ppermute(array, axis_name, [(i, i ^ k) for i in range(size)]) for k in range(1, size)
    ]


def in_order(parts, index):
    step = 1
    parts = list(parts)
    while step < len(parts):
        turned = index // step % 2 == 1
        for k in range(len(parts)):
            if k & step == 0:
                low, high = parts[k], parts[k + step]
                parts[k], parts[k + step] = jnp.where(turned, high, low), jnp.where(turned, low, high)
        step *= 2
    return parts


def axis_join(piece, axis_name, dim=0):
    return jnp.concatenate(in_order(others(piece, axis_name), lax.axis_index(axis_name)), dim)


def group_sum(small):
    return (
        small + swap(small, "zl") + swap(small, "core") + lax.ppermute(small, GROUP, CROSS)
    )


def core_sum(small):
    return small + swap(small, "core")


def ordered(mine, other, axis_name, dim):
    first = lax.axis_index(axis_name) == 0
    return jnp.where(
        first, jnp.concatenate([mine, other], dim), jnp.concatenate([other, mine], dim)
    )


def join(piece, axis_name, dim):
    return ordered(piece, swap(piece, axis_name), axis_name, dim)


def halves(whole, axis_name, dim):
    low, high = jnp.split(whole, 2, dim)
    first = lax.axis_index(axis_name) == 0
    return jnp.where(first, low, high), jnp.where(first, high, low)


def trade(whole, axis_name, cut, lay):
    keep, give = halves(whole, axis_name, cut)
    return ordered(keep, swap(give, axis_name), axis_name, lay)


def scatter_sum(partial, axis_name, dim):
    keep, give = halves(partial, axis_name, dim)
    return keep.astype(f32) + swap(give.astype(bf16), axis_name).astype(f32)


def by_seq(rows):
    return rows.reshape(2, rows.shape[0] // 2, rows.shape[1])


def flat(rows):
    return rows.reshape(-1, rows.shape[-1])


def layer_norm(values):
    centred = values - jnp.mean(values, axis=-1, keepdims=True)
    inv = lax.rsqrt(jnp.mean(centred * centred, axis=-1, keepdims=True) + NORM_EPS)
    return centred * inv, inv


def split_norm(values):
    local = values.shape[1]
    mean_here = jnp.mean(values, axis=-1)
    centred = values - mean_here[:, None]
    mine = jnp.stack([mean_here, jnp.sum(centred * centred, axis=-1)])
    other = swap(mine, "core")
    mean = (mine[0] + other[0]) / 2
    apart = mine[0] - mean
    spread = mine[1] + other[1] + 2 * local * apart * apart
    inv = lax.rsqrt(spread / (2 * local) + NORM_EPS)
    return (values - mean[:, None]) * inv[:, None], inv


def turn(values, cos, sin):
    lanes = lax.broadcasted_iota(jnp.int32, values.shape, 1)
    swapped = jnp.where(
        lanes % 2 == 0,
        -pltpu.roll(values, HEAD_DIM - 1, 1),
        pltpu.roll(values, 1, 1),
    )
    return values * cos + swapped * sin


def attend(query, key):
    scores = mm_nt(query, key) * SCALE
    peak = jnp.max(scores, axis=-1, keepdims=True)
    weights = jnp.exp(scores - peak)
    weights = weights / jnp.sum(weights, axis=-1, keepdims=True)
    return weights


def attend_grads(query, key, value, grad):
    weights = attend(query, key)
    grad_weights = mm_nt(grad, value)
    delta = jnp.sum(weights * grad_weights, axis=-1, keepdims=True)
    grad_scores = (weights * (grad_weights - delta)).astype(bf16)
    grad_query = mm(grad_scores, key) * SCALE
    grad_key = mm_tn(grad_scores, query) * SCALE
    grad_value = mm_tn(weights.astype(bf16), grad)
    return grad_query, grad_key, grad_value


def self_forward_kernel(q_ref, k_ref, v_ref, r_ref, gq_ref, gk_ref, cos_ref, sin_ref,
                        qr_ref, kr_ref, vb_ref, o_ref):
    cos, sin = cos_ref[...], sin_ref[...]
    query = turn(q_ref[...] * r_ref[:, 0:1] * gq_ref[...], cos, sin).astype(bf16)
    key = turn(k_ref[...] * r_ref[:, 1:2] * gk_ref[...], cos, sin).astype(bf16)
    value = v_ref[...].astype(bf16)
    qr_ref[...] = query
    kr_ref[...] = key
    vb_ref[...] = value
    weights = attend(query, key).astype(bf16)
    o_ref[...] = mm(weights, value).astype(bf16)


def self_forward(qkv, inverse, gain_q, gain_k, cos, sin, clips):
    rows, local = qkv.shape[0], qkv.shape[1] // 3
    heads, tokens = local // HEAD_DIM, rows // clips

    def at(shift):
        return pl.BlockSpec((tokens, HEAD_DIM), lambda b, h, s=shift: (b, h + s))

    gain = pl.BlockSpec((1, HEAD_DIM), lambda b, h: (0, h))
    table = pl.BlockSpec((tokens, HEAD_DIM), lambda b, h: (b, 0))
    return pl.pallas_call(
        self_forward_kernel,
        grid=(clips, heads),
        in_specs=[at(0), at(heads), at(2 * heads),
                  pl.BlockSpec((tokens, 2), lambda b, h: (b, 0)), gain, gain, table, table],
        out_specs=[at(0)] * 4,
        out_shape=[jax.ShapeDtypeStruct((rows, local), bf16)] * 4,
        cost_estimate=pl.CostEstimate(flops=8 * 10**9, bytes_accessed=10**7, transcendentals=10**6),
        name="self_forward",
    )(qkv, qkv, qkv, inverse, gain_q, gain_k, cos, sin)


def self_backward_kernel(qr_ref, kr_ref, vb_ref, do_ref, q_ref, k_ref, r_ref, gq_ref, gk_ref,
                         cos_ref, sin_ref, uq_ref, uk_ref, dv_ref, part_ref, dgain_ref):
    cos, sin = cos_ref[...], sin_ref[...]
    grad_query, grad_key, grad_value = attend_grads(
        qr_ref[...], kr_ref[...], vb_ref[...], do_ref[...]
    )
    up_q = turn(grad_query, cos, -sin)
    up_k = turn(grad_key, cos, -sin)
    dv_ref[...] = grad_value.astype(bf16)
    vq, vk = up_q * q_ref[...], up_k * k_ref[...]
    dgain_ref[0, 0, 0:1, :] = jnp.sum(vq * r_ref[:, 0:1], axis=0, keepdims=True)
    dgain_ref[0, 0, 1:2, :] = jnp.sum(vk * r_ref[:, 1:2], axis=0, keepdims=True)
    up_q, up_k = up_q * gq_ref[...], up_k * gk_ref[...]
    uq_ref[...] = up_q
    uk_ref[...] = up_k
    mean_q = jnp.sum(vq * gq_ref[...], axis=-1, keepdims=True)
    mean_k = jnp.sum(vk * gk_ref[...], axis=-1, keepdims=True)
    both = jnp.concatenate([mean_q, mean_k], axis=1)

    @pl.when(pl.program_id(1) == 0)
    def _():
        part_ref[...] = both

    @pl.when(pl.program_id(1) > 0)
    def _():
        part_ref[...] += both


def self_backward(qr, kr, vb, grad, qkv, inverse, gain_q, gain_k, cos, sin, clips):
    rows, local = qr.shape
    heads, tokens = local // HEAD_DIM, rows // clips

    def at(shift):
        return pl.BlockSpec((tokens, HEAD_DIM), lambda b, h, s=shift: (b, h + s))

    gain = pl.BlockSpec((1, HEAD_DIM), lambda b, h: (0, h))
    table = pl.BlockSpec((tokens, HEAD_DIM), lambda b, h: (b, 0))
    pair = pl.BlockSpec((tokens, 2), lambda b, h: (b, 0))
    return pl.pallas_call(
        self_backward_kernel,
        grid=(clips, heads),
        in_specs=[at(0)] * 4 + [at(0), at(heads), pair, gain, gain, table, table],
        out_specs=[at(0)] * 3 + [pair, pl.BlockSpec((1, 1, 2, HEAD_DIM), lambda b, h: (b, h, 0, 0))],
        out_shape=[
            jax.ShapeDtypeStruct((rows, local), f32),
            jax.ShapeDtypeStruct((rows, local), f32),
            jax.ShapeDtypeStruct((rows, local), bf16),
            jax.ShapeDtypeStruct((rows, 2), f32),
            jax.ShapeDtypeStruct((clips, heads, 2, HEAD_DIM), f32),
        ],
        cost_estimate=pl.CostEstimate(flops=11 * 10**9, bytes_accessed=10**7, transcendentals=10**6),
        name="self_backward",
    )(qr, kr, vb, grad, qkv, qkv, inverse, gain_q, gain_k, cos, sin)


def cross_forward_kernel(q_ref, r_ref, g_ref, k_ref, v_ref, qn_ref, o_ref):
    tokens, words = q_ref.shape[0] // 2, k_ref.shape[0] // 2
    for clip in range(2):
        rows, text = pl.ds(clip * tokens, tokens), pl.ds(clip * words, words)
        query = (q_ref[rows, :] * r_ref[rows, :] * g_ref[...]).astype(bf16)
        qn_ref[rows, :] = query
        weights = attend(query, k_ref[text, :]).astype(bf16)
        o_ref[rows, :] = mm(weights, v_ref[text, :]).astype(bf16)


def cross_forward(cq, inverse, gain, key, value):
    rows, local = cq.shape
    at = pl.BlockSpec((rows, HEAD_DIM), lambda h: (0, h))
    text = pl.BlockSpec((key.shape[0], HEAD_DIM), lambda h: (0, h))
    return pl.pallas_call(
        cross_forward_kernel,
        grid=(local // HEAD_DIM,),
        in_specs=[at, pl.BlockSpec((rows, 1), lambda h: (0, 0)),
                  pl.BlockSpec((1, HEAD_DIM), lambda h: (0, h)), text, text],
        out_specs=[at, at],
        out_shape=[jax.ShapeDtypeStruct((rows, local), bf16)] * 2,
        cost_estimate=pl.CostEstimate(flops=9 * 10**9, bytes_accessed=10**7, transcendentals=10**6),
        name="cross_forward",
    )(cq, inverse, gain, key, value)


def cross_backward_kernel(qn_ref, k_ref, v_ref, do_ref, dq_ref, dk_ref, dv_ref):
    tokens, words = qn_ref.shape[0] // 2, k_ref.shape[0] // 2
    for clip in range(2):
        rows, text = pl.ds(clip * tokens, tokens), pl.ds(clip * words, words)
        grad_query, grad_key, grad_value = attend_grads(
            qn_ref[rows, :], k_ref[text, :], v_ref[text, :], do_ref[rows, :]
        )
        dq_ref[rows, :] = grad_query
        dk_ref[text, :] = grad_key
        dv_ref[text, :] = grad_value.astype(bf16)


def cross_backward(query, key, value, grad):
    rows, local = query.shape
    at = pl.BlockSpec((rows, HEAD_DIM), lambda h: (0, h))
    text = pl.BlockSpec((key.shape[0], HEAD_DIM), lambda h: (0, h))
    return pl.pallas_call(
        cross_backward_kernel,
        grid=(local // HEAD_DIM,),
        in_specs=[at, text, text, at],
        out_specs=[at, text, text],
        out_shape=[
            jax.ShapeDtypeStruct((rows, local), f32),
            jax.ShapeDtypeStruct(key.shape, f32),
            jax.ShapeDtypeStruct(key.shape, bf16),
        ],
        cost_estimate=pl.CostEstimate(flops=11 * 10**9, bytes_accessed=10**7, transcendentals=10**6),
        name="cross_backward",
    )(query, key, value, grad)


PACK = 256
REST = 768
GELU_A = 0.7978845608028654
GELU_B = 0.044715


def mlp_kernel(core_ref, x_ref, xo_ref, g_ref, go_ref, pack_ref, act_ref, gh_ref, gx_ref, gxo_ref,
               up, down, act, gh, total, total_other, sems, out_sems):
    peers, up_rows, hidden = up.shape
    down_rows, width = down.shape[1:]
    half = width // 2
    cuts = [0, hidden // PACK // 2 * PACK, hidden]
    loads, last = [], 0
    for k in range(2):
        first, last = last, -(-cuts[k + 1] // down_rows)
        moves = [
            (pack_ref.at[:, pl.ds(at // PACK * up_rows, up_rows), :], up.at[:, :, pl.ds(at, PACK)])
            for at in range(cuts[k], cuts[k + 1], PACK)
        ]
        for at in range(0, width, PACK):
            line = hidden // PACK * up_rows + at // PACK * down_rows
            moves.append(
                (
                    pack_ref.at[pl.ds(first, last - first), pl.ds(line, down_rows), :],
                    down.at[pl.ds(first, last - first), :, pl.ds(at, PACK)],
                )
            )
        loads.append([pltpu.make_async_copy(*m, sems.at[k, i]) for i, m in enumerate(moves)])
        for copy in loads[-1]:
            copy.start()
    down_flat = down.reshape(peers * down_rows, width)
    up_flat = up.reshape(peers * up_rows, hidden)
    mine = pl.ds(pl.multiple_of(core_ref[0] * half, half), half)
    other = pl.ds(pl.multiple_of((1 - core_ref[0]) * half, half), half)
    stores = []
    for k in range(2):
        for copy in loads[k]:
            copy.wait()
        cols = pl.ds(cuts[k], cuts[k + 1] - cuts[k])
        pre = mm(x_ref[...], up_flat[mine, cols]) + mm(xo_ref[...], up_flat[other, cols])
        grad = mm_nt(g_ref[...], down_flat[cols, mine]) + mm_nt(go_ref[...], down_flat[cols, other])
        square = pre * pre
        tanh = jnp.tanh(GELU_A * pre * (1.0 + GELU_B * square))
        share = 0.5 * (1.0 + tanh)
        act[:, cols] = (pre * share).astype(bf16)
        slope = share + pre * (0.5 * GELU_A) * (1.0 - tanh * tanh) * (1.0 + 3 * GELU_B * square)
        grad = (grad * slope).astype(bf16)
        gh[:, cols] = grad
        for i, (here, there) in enumerate(((act, act_ref), (gh, gh_ref))):
            stores.append(pltpu.make_async_copy(here.at[:, cols], there.at[:, cols], out_sems.at[k, i]))
            stores[-1].start()
        for rows, sums, out in ((mine, total, gx_ref), (other, total_other, gxo_ref)):
            part = mm_nt(grad, up_flat[rows, cols])
            if k == 0:
                sums[...] = part
            else:
                out[...] = (sums[...] + part).astype(bf16)
    for copy in stores:
        copy.wait()


def mlp(core, inputs, grads, packed, up_rows, hidden, down_rows):
    rows, half = inputs[0].shape
    width = 2 * half
    peers = packed.shape[0]
    copies = -(-hidden // PACK // 2) + width // PACK
    vmem = pl.BlockSpec(memory_space=pltpu.VMEM)
    any_space = pl.BlockSpec(memory_space=pl.ANY)
    return pl.pallas_call(
        mlp_kernel,
        in_specs=[pl.BlockSpec(memory_space=pltpu.SMEM)] + [vmem] * 4 + [any_space],
        out_specs=[any_space, any_space, vmem, vmem],
        out_shape=[
            jax.ShapeDtypeStruct((rows, hidden), bf16),
            jax.ShapeDtypeStruct((rows, hidden), bf16),
            jax.ShapeDtypeStruct((rows, half), bf16),
            jax.ShapeDtypeStruct((rows, half), bf16),
        ],
        scratch_shapes=[
            pltpu.VMEM((peers, up_rows, hidden), bf16),
            pltpu.VMEM((peers, down_rows, width), bf16),
            pltpu.VMEM((rows, hidden), bf16),
            pltpu.VMEM((rows, hidden), bf16),
            pltpu.VMEM((rows, half), f32),
            pltpu.VMEM((rows, half), f32),
            pltpu.SemaphoreType.DMA((2, copies)),
            pltpu.SemaphoreType.DMA((2, 2)),
        ],
        compiler_params=pltpu.CompilerParams(vmem_limit_bytes=56 * 2**20),
        cost_estimate=pl.CostEstimate(
            flops=6 * rows * width * hidden, bytes_accessed=packed.size * 2, transcendentals=rows * hidden
        ),
        name="mlp",
    )(core, *inputs, *grads, packed)


def tn_pack_kernel(place, x_ref, g_ref, *rest):
    pack_ref, held, sems = rest[-3:]
    peers, rows, _ = held.shape[1:]
    slots = held.shape[0]
    copies = []
    for k in range(slots):
        grad = g_ref[:, k * REST : (k + 1) * REST]
        lines = held.at[k].reshape(peers * rows, REST)
        lines[...] = mm_tn(x_ref[...], grad).astype(bf16)
        copies.append(
            pltpu.make_async_copy(
                held.at[k], pack_ref.at[:, pl.ds((place + k) * rows, rows), :], sems.at[k]
            )
        )
        copies[-1].start()
    for copy in copies:
        copy.wait()


def tn_pack(left, right, place, places, peers, packed=None):
    width, slots = left.shape[1], right.shape[1] // REST
    rows = width // peers
    vmem = pl.BlockSpec(memory_space=pltpu.VMEM)
    any_space = pl.BlockSpec(memory_space=pl.ANY)
    given = [] if packed is None else [packed]
    return pl.pallas_call(
        functools.partial(tn_pack_kernel, place),
        in_specs=[vmem, vmem] + [any_space] * len(given),
        out_specs=any_space,
        out_shape=jax.ShapeDtypeStruct((peers, places * rows, REST), bf16),
        scratch_shapes=[pltpu.VMEM((slots, peers, rows, REST), bf16), pltpu.SemaphoreType.DMA((slots,))],
        input_output_aliases={2: 0} if given else {},
        compiler_params=pltpu.CompilerParams(vmem_limit_bytes=56 * 2**20),
        cost_estimate=pl.CostEstimate(
            flops=2 * left.size * right.shape[1], bytes_accessed=2 * width * right.shape[1], transcendentals=0
        ),
        name="tn_pack",
    )(left, right, *given)


def mlp_grads_kernel(core_ref, x_ref, xo_ref, gh_ref, act_ref, g_ref, go_ref, pack_ref, up, down, up_sems, down_sems):
    copies = []
    blocks, peers, rows, _ = up.shape
    some = peers // 2
    line = blocks * rows
    for part, left in enumerate((x_ref, xo_ref)):
        first = core_ref[0] if part == 0 else 1 - core_ref[0]
        grad = mm_tn(left[...], gh_ref[...]).astype(bf16)
        for k in range(blocks):
            held = up.at[k, pl.ds(part * some, some)]
            held[...] = grad[:, k * PACK : (k + 1) * PACK].reshape(some, rows, PACK)
            there = pack_ref.at[pl.ds(first * some, some), pl.ds(k * rows, rows), :]
            copies.append(pltpu.make_async_copy(held, there, up_sems.at[part, k]))
            copies[-1].start()
    blocks, _, rows, _ = down.shape
    for part, right in enumerate((g_ref, go_ref)):
        first = core_ref[0] if part == 0 else 1 - core_ref[0]
        grad = mm_tn(act_ref[...], right[...]).astype(bf16)
        for k in range(blocks // 2):
            held = down.at[part * (blocks // 2) + k]
            held[...] = grad[:, k * PACK : (k + 1) * PACK].reshape(peers, rows, PACK)
            at = pl.multiple_of(line + (first * (blocks // 2) + k) * rows, 16)
            there = pack_ref.at[:, pl.ds(at, rows), :]
            copies.append(pltpu.make_async_copy(held, there, down_sems.at[part, k]))
            copies[-1].start()
    for copy in copies:
        copy.wait()


def mlp_grads(core, inputs, grad_hidden, activated, grads, peers):
    width, hidden = 2 * inputs[0].shape[1], activated.shape[1]
    up_rows, down_rows = width // peers, hidden // peers
    lines = hidden // PACK * up_rows + width // PACK * down_rows
    vmem = pl.BlockSpec(memory_space=pltpu.VMEM)
    return pl.pallas_call(
        mlp_grads_kernel,
        in_specs=[pl.BlockSpec(memory_space=pltpu.SMEM)] + [vmem] * 6,
        out_specs=pl.BlockSpec(memory_space=pl.ANY),
        out_shape=jax.ShapeDtypeStruct((peers, lines, PACK), bf16),
        scratch_shapes=[
            pltpu.VMEM((hidden // PACK, peers, up_rows, PACK), bf16),
            pltpu.VMEM((width // PACK, peers, down_rows, PACK), bf16),
            pltpu.SemaphoreType.DMA((2, hidden // PACK)),
            pltpu.SemaphoreType.DMA((2, width // PACK // 2)),
        ],
        compiler_params=pltpu.CompilerParams(vmem_limit_bytes=56 * 2**20),
        cost_estimate=pl.CostEstimate(
            flops=4 * width * inputs[0].shape[0] * hidden, bytes_accessed=4 * width * hidden, transcendentals=0
        ),
        name="mlp_grads",
    )(core, *inputs, grad_hidden, activated, *grads)


def tail_kernel(places, at_ref, x_ref, g_ref, w_ref, n_ref, small_ref, first_ref, second_ref, keep_ref, give_ref, held):
    cut, some = first_ref.shape[1], x_ref.shape[0] // 2
    ones = jnp.ones((x_ref.shape[0], 128), bf16)
    part = mm_nt(g_ref[...], w_ref[...])
    low = part.astype(bf16)
    shift = mm_tn(low, ones)
    scale = mm_tn((part * n_ref[...].astype(f32)).astype(bf16), ones)
    lane = lax.broadcasted_iota(jnp.int32, shift.shape, 1)
    small = jnp.where(lane == 6, shift, jnp.where(lane == 7, scale, small_ref[...]))
    held[...] = small.astype(bf16)
    zero = at_ref[0] == 0
    keep_ref[...] = jnp.where(zero, low[:some], low[some:])
    give_ref[...] = jnp.where(zero, low[some:], low[:some])
    down, across = places
    lines = x_ref.shape[1] // (down * across)
    step = down * across // 2
    for k in range(2):
        rows = pl.ds(k * step * lines, step * lines)
        grad = mm_tn(x_ref[:, rows], g_ref[...]).astype(bf16)
        for i in range(step):
            y, x = divmod(k * step + i, across)
            y = y ^ at_ref[1]
            here = slice(i * lines, (i + 1) * lines)
            there = pl.ds(pl.multiple_of((x * down + y) * lines, 16), lines)
            first_ref[there, :] = grad[here, :cut]
            there = pl.ds(pl.multiple_of((y * across + x) * lines, 16), lines)
            second_ref[there, : g_ref.shape[1] - cut] = grad[here, cut:]
            second_ref[there, g_ref.shape[1] - cut :] = held[pl.ds((k * step + i) * lines, lines), :]


def tail(places, at, inputs, grad, weight, norm, small):
    rows, width = inputs.shape
    cut = (grad.shape[1] + 128) // 2
    out = [
        jax.ShapeDtypeStruct((width, cut), bf16),
        jax.ShapeDtypeStruct((width, cut), bf16),
        jax.ShapeDtypeStruct((rows // 2, width), bf16),
        jax.ShapeDtypeStruct((rows // 2, width), bf16),
    ]

    def first_block(shape):
        return pl.BlockSpec(shape, lambda i: (0, 0))

    return pl.pallas_call(
        functools.partial(tail_kernel, places),
        grid=(1,),
        in_specs=[pl.BlockSpec(memory_space=pltpu.SMEM)]
        + [first_block(s) for s in (inputs.shape, grad.shape, (width, grad.shape[1]), norm.shape, small.shape)],
        out_specs=[first_block(o.shape) for o in out],
        out_shape=out,
        scratch_shapes=[pltpu.VMEM((width, 128), bf16)],
        compiler_params=pltpu.CompilerParams(vmem_limit_bytes=56 * 2**20),
        cost_estimate=pl.CostEstimate(flops=8 * 10**9, bytes_accessed=10**7, transcendentals=0),
        name="tail",
    )(at, inputs, grad, weight, norm, small)


def inverse_freq(pair_total):
    return 1.0 / 10000.0 ** (jnp.arange(pair_total, dtype=f32) * 2.0 / (2.0 * pair_total))


def rotary_tables(places):
    pair_count = HEAD_DIM // 2
    side = pair_count // 3
    frame = pair_count - 2 * side
    freq = jnp.concatenate([inverse_freq(frame), inverse_freq(side), inverse_freq(side)])
    freq = jnp.repeat(freq, 2)[None, :]
    pair = lax.broadcasted_iota(jnp.int32, (1, HEAD_DIM), 1) // 2
    angles = jnp.where(
        pair < frame,
        places[0][:, None],
        jnp.where(pair < frame + side, places[1][:, None], places[2][:, None]),
    ) * freq
    return jnp.cos(angles), jnp.sin(angles)


def columns_for(weight, count, owners):
    rows = weight.shape[0]
    parts = jnp.transpose(weight.reshape(rows, count, owners, -1), (2, 0, 1, 3))
    return parts.reshape(owners, rows, -1)


def along_line(parts):
    return lax.all_to_all(parts, LINE, split_axis=0, concat_axis=0, tiled=True)


def for_line(group_parts=None, core_parts=None):
    if core_parts is not None:
        group_parts = jnp.repeat(core_parts, 2, axis=0)
    return jnp.concatenate([group_parts, group_parts], 0)


def first_then(first, *then):
    return lax.optimization_barrier((first, *then))[1:]


def on_device(
    latent_tokens, time_embed, text_tokens, positions,
    w_qkv, attn_out, cross_q, cross_kv, cross_out, mlp_in, mlp_out,
    gain_q, gain_k, gain_cq, gain_ck, norm_weight, norm_bias, modulation, cotangent,
):
    peers = lax.axis_size(PLACES)
    core, zl = lax.axis_index("core"), lax.axis_index("zl")
    width = latent_tokens.shape[2]
    half, local = width // 2, width // 4
    clips = 2
    rows_each = w_qkv.shape[0]
    line_rows = 8 * rows_each
    hid_each = mlp_out.shape[0]
    hid_pad = -(-hid_each * peers // 256) * 256 // peers
    hidden = peers * hid_pad

    x_mine = latent_tokens[0]
    x_wide = join(join(x_mine, "zl", 0), "core", 0)
    text = join(join(text_tokens[0], "zl", 0), "core", 0)
    small = jnp.concatenate(
        [v[None] for v in (gain_q, gain_k, gain_cq, gain_ck, norm_weight, norm_bias)] + [modulation], 0
    )
    small = jnp.pad(small.T, ((0, 0), (0, 116)))
    shard = along_line(
        jnp.concatenate(
            [
                for_line(group_parts=columns_for(w_qkv, 3, 4)),
                for_line(core_parts=columns_for(attn_out, 1, 2)),
                jnp.broadcast_to(small, (8, *small.shape)),
            ],
            axis=2,
        )
    ).reshape(line_rows, -1)
    first_weight = lax.all_gather(shard[:, : 3 * local + half], PLACES, axis=0, tiled=True)
    qkv_weight, out_weight = first_weight[:, : 3 * local], first_weight[:, 3 * local :]
    whole = shard[:, 3 * local + half : 3 * local + half + 12].T.reshape(1, -1)
    whole = axis_join(axis_join(whole, "x"), "y").reshape(peers, 12, line_rows)
    whole = jnp.transpose(whole, (1, 0, 2)).reshape(12, width).astype(f32)

    parts = jnp.concatenate(
        [columns_for(cross_q, 1, 2), columns_for(cross_kv, 2, 2), columns_for(cross_out, 1, 2)], axis=2
    )
    whole, parts = lax.optimization_barrier((whole, parts))
    cross_shard = along_line(for_line(core_parts=parts)).reshape(line_rows, -1)
    cross_weight = lax.all_gather(cross_shard, PLACES, axis=0, tiled=True)
    cq_weight = cross_weight[:, :half]
    ckv_weight = cross_weight[:, half : 3 * half]
    co_weight = cross_weight[:, 3 * half :]

    time_rows = join(time_embed, "core", 0)
    mod_wide = time_rows + whole[None, 6:]
    mod_mine = time_embed[0] + whole[6:]

    def here(rows, cut):
        picked = jnp.split(rows, 2, -1)
        rows = jnp.where(core == 0, picked[0], picked[1])
        if cut == 4:
            picked = jnp.split(rows, 2, -1)
            rows = jnp.where(zl == 0, picked[0], picked[1])
        return rows

    mod = here(mod_wide, 2)
    g_q, g_k = here(whole[0:1], 4), here(whole[1:2], 4)
    g_cq, g_ck, n_w, n_b = (here(whole[i : i + 1], 2) for i in range(2, 6))
    tokens = latent_tokens.shape[1]

    def per_clip(row):
        rows = mod[:, row]
        return jnp.broadcast_to(rows[:, None], (clips, tokens, half)).reshape(-1, half)

    places = join(join(positions[0].astype(f32), "zl", 1), "core", 1)
    cos, sin = rotary_tables(places)
    x_here = trade(x_mine, "core", 1, 0).astype(f32)
    up_here = trade(cotangent[0], "core", 1, 0).astype(f32)
    norm_wide, _ = layer_norm(x_wide.astype(f32))
    attn_input = norm_wide.reshape(clips, -1, width) * (1.0 + mod_wide[:, 1:2]) + mod_wide[:, 0:1]
    attn_input = flat(attn_input).astype(bf16)
    attn_input, text, x_here, up_here = lax.optimization_barrier((attn_input, text, x_here, up_here))

    qkv = mm(attn_input, qkv_weight)
    squares = jnp.sum((qkv * qkv).reshape(-1, 3, local)[:, :2], axis=-1).T
    inv_qk = lax.rsqrt(group_sum(squares) / width + NORM_EPS).T
    qr, kr, vb, heads = self_forward(qkv, inv_qk, g_q, g_k, cos, sin, clips)
    heads = flat(trade(heads.reshape(2, -1, local), "zl", 1, 2))
    attn_tokens = join(heads, "core", 1)

    up = mlp_in.reshape(rows_each, peers, 8, hid_each)
    up = jnp.pad(up, ((0, 0), (0, 0), (0, 0), (0, hid_pad - hid_each)))
    up = jnp.transpose(up, (2, 0, 1, 3)).reshape(8, rows_each, hidden)
    attn_tokens, up = lax.optimization_barrier((attn_tokens, up))
    up_shard = along_line(up).reshape(line_rows, hidden)
    down = jnp.pad(mlp_out, ((0, hid_pad - hid_each), (0, 0)))
    mlp_shard = jnp.concatenate(
        [up_shard[:, at : at + PACK] for at in range(0, hidden, PACK)]
        + [down[:, at : at + PACK] for at in range(0, width, PACK)],
        axis=0,
    )
    mlp_pack = lax.all_gather(mlp_shard, PLACES, axis=0)

    branch_one = mm(attn_tokens, out_weight)
    after_attn = x_here + branch_one * per_clip(2)
    norm_two, inv_two = split_norm(after_attn)
    cross_input = join((norm_two * n_w + n_b).astype(bf16), "core", 1)
    grad_three = (up_here * per_clip(5)).astype(bf16)
    cross_input, grad_three = lax.optimization_barrier((cross_input, grad_three))
    grad_three = others(grad_three, CHIPS)

    ckv = mm(text, ckv_weight)
    ck_pre = ckv[:, :half]
    inv_ck = lax.rsqrt(core_sum(jnp.sum(ck_pre * ck_pre, axis=-1)[None]) / width + NORM_EPS)[0]
    cross_key = (ck_pre * inv_ck[:, None] * g_ck).astype(bf16)
    cross_value = ckv[:, half:].astype(bf16)
    cq_pre = mm(cross_input, cq_weight)
    inv_cq = lax.rsqrt(core_sum(jnp.sum(cq_pre * cq_pre, axis=-1)[None]) / width + NORM_EPS)[0]
    cross_query, cross_heads = cross_forward(cq_pre, inv_cq[:, None], g_cq, cross_key, cross_value)
    cross_heads, *grad_three = lax.optimization_barrier((cross_heads, *grad_three))

    def both_cores(pieces):
        lines = jnp.concatenate(pieces, 0)
        return lines, swap(lines, "core")

    grad_three = both_cores(grad_three)
    cross_tokens = join(cross_heads, "core", 1)
    after_cross = after_attn + mm(cross_tokens, co_weight)

    norm_three, inv_three = split_norm(after_cross)
    mlp_input = (norm_three * (1.0 + per_clip(4)) + per_clip(3)).astype(bf16)
    mlp_input = both_cores(others(mlp_input, CHIPS))
    core_row = jnp.full((1,), core, jnp.int32)
    activated, grad_hidden, keep, give = mlp(
        core_row, mlp_input, grad_three, mlp_pack, line_rows, hidden, hid_pad
    )

    def to_near(blocks):
        return [lax.ppermute(blocks[k], CHIPS, [(i, i ^ (k + 1)) for i in range(4)]) for k in range(3)]

    def core_lines(keep, give):
        lines = keep.astype(f32) + swap(give, "core").astype(f32)
        return lines[: 2 * tokens], jnp.split(lines[2 * tokens :].astype(bf16), 3, 0)

    near_input, far = core_lines(keep, give)
    down_weight = jnp.concatenate(
        [
            mlp_pack[:, at : at + hid_pad].reshape(hidden, PACK)
            for at in range(line_rows * (hidden // PACK), mlp_pack.shape[1], hid_pad)
        ],
        axis=1,
    )
    near, three = core_lines(*halves(mm(activated, down_weight).astype(bf16), "core", 1))
    activated, grad_hidden, *far = lax.optimization_barrier((activated, grad_hidden, *far))
    far = to_near(far)
    mlp_lines = mlp_grads(core_row, mlp_input, grad_hidden, activated, grad_three, peers)
    mlp_lines, *far = lax.optimization_barrier((mlp_lines, *far))
    grad_mlp_input = near_input + sum(part.astype(f32) for part in far)
    mlp_lines = mlp_lines.reshape(-1, PACK)
    mlp_sum = lax.psum_scatter(mlp_lines, PLACES, scatter_dimension=0, tiled=True)

    def norm_back(grad, scaled, norm, inv):
        sums = core_sum(jnp.stack([jnp.sum(scaled, axis=-1), jnp.sum(scaled * norm, axis=-1)])) / width
        return (scaled - sums[0][:, None] - norm * sums[1][:, None]) * inv[:, None]

    grad_mod3 = jnp.sum(grad_mlp_input, axis=0)
    grad_mod4 = jnp.sum(grad_mlp_input * norm_three, axis=0)
    grad_cross = up_here + norm_back(
        grad_mlp_input, grad_mlp_input * (1.0 + per_clip(4)), norm_three, inv_three
    )
    grad_two = grad_cross.astype(bf16)

    grad_heads = scatter_sum(mm_nt(grad_two, co_weight).astype(bf16), "core", 1).astype(bf16)
    rest_lines = tn_pack(cross_tokens, grad_two, 4, 5, peers)
    grad_heads, near, *three = lax.optimization_barrier((grad_heads, near, *three))
    three = to_near(three)
    up_cq, up_ck, up_cv = cross_backward(cross_query, cross_key, cross_value, grad_heads)
    up_cq, *three = lax.optimization_barrier((up_cq, *three))
    branch_three = near + sum(part.astype(f32) for part in three)
    result_here = (after_cross + branch_three * per_clip(5)).astype(bf16)
    grad_mod5 = jnp.sum(up_here * branch_three, axis=0)
    result = trade(result_here, "core", 0, 1)

    def rms_back(grad, pre, inv, gain):
        mean = core_sum(jnp.sum(grad * pre * gain, axis=-1)[None])[0] / width
        gain_grad = jnp.sum(grad * pre * inv[:, None], axis=0)
        return (grad * gain - pre * (inv * inv * mean)[:, None]) * inv[:, None], gain_grad

    grad_cq, grad_gain_cq = rms_back(up_cq, cq_pre, inv_cq, g_cq)
    grad_cq = grad_cq.astype(bf16)
    grad_cross_input = scatter_sum(mm_nt(grad_cq, cq_weight).astype(bf16), "core", 1)
    grad_ck, grad_gain_ck = rms_back(up_ck, ck_pre, inv_ck, g_ck)
    grad_ckv = jnp.concatenate([grad_ck.astype(bf16), up_cv], axis=1)
    rest_lines = tn_pack(cross_input, grad_cq, 1, 5, peers, rest_lines)
    rest_lines = tn_pack(text, grad_ckv, 2, 5, peers, rest_lines)
    grad_n_w = jnp.sum(grad_cross_input * norm_two, axis=0)
    grad_n_b = jnp.sum(grad_cross_input, axis=0)
    grad_attn = grad_cross + norm_back(grad_cross_input, grad_cross_input * n_w, norm_two, inv_two)
    grad_attn_mine = trade(grad_attn, "core", 0, 1)

    grad_one = (grad_attn * per_clip(2)).astype(bf16)
    grad_mod2 = jnp.sum(grad_attn * branch_one, axis=0)
    grad_heads = scatter_sum(mm_nt(grad_one, out_weight).astype(bf16), "core", 1).astype(bf16)
    grad_heads = flat(trade(by_seq(grad_heads), "zl", 2, 1))
    rest_lines = tn_pack(attn_tokens, grad_one, 0, 5, peers, rest_lines)
    mlp_sum, rest_lines = lax.optimization_barrier((mlp_sum, rest_lines))
    rest_sum = lax.psum_scatter(rest_lines.reshape(-1, REST), PLACES, scatter_dimension=0, tiled=True)
    up_q, up_k, grad_v, part, dgain = self_backward(
        qr, kr, vb, grad_heads, qkv, inv_qk, g_q, g_k, cos, sin, clips
    )
    mean_qk = group_sum(part.T) / width
    pull = (mean_qk * (inv_qk * inv_qk).T).T
    grad_q = (up_q - qkv[:, :local] * pull[:, 0:1]) * inv_qk[:, 0:1]
    grad_k = (up_k - qkv[:, local : 2 * local] * pull[:, 1:2]) * inv_qk[:, 1:2]
    grad_qkv = jnp.concatenate([grad_q.astype(bf16), grad_k.astype(bf16), grad_v], axis=1)
    dgain = jnp.transpose(jnp.sum(dgain, axis=0), (1, 0, 2)).reshape(2, local)

    dgain = jnp.where(zl == 0, jnp.pad(dgain, ((0, 0), (0, local))), jnp.pad(dgain, ((0, 0), (local, 0))))
    halfs = jnp.concatenate(
        [
            dgain,
            jnp.stack(
                [
                    grad_gain_cq, grad_gain_ck, grad_n_w, grad_n_b,
                    jnp.zeros_like(grad_n_b), jnp.zeros_like(grad_n_b),
                    grad_mod2, grad_mod3, grad_mod4, grad_mod5,
                ]
            ),
        ],
        0,
    )
    smalls = jnp.where(
        core == 0, jnp.pad(halfs, ((0, 0), (0, half))), jnp.pad(halfs, ((0, 0), (half, 0)))
    )
    small_cols = jnp.pad(smalls.T, ((0, 0), (0, 116)))
    down_across = (lax.axis_size("y"), lax.axis_size("x"))
    at_row = jnp.stack([core, lax.axis_index("y")]).astype(jnp.int32)
    *last_lines, keep, give = tail(
        down_across, at_row, attn_input, grad_qkv, first_weight, norm_wide.astype(bf16), small_cols
    )

    def sum_both(by_x, by_y):
        by_x = by_x.reshape(down_across[1], -1, by_x.shape[-1])
        by_y = jnp.split(by_y, down_across[0], 0)
        from_x = lax.all_to_all(by_x, "x", split_axis=0, concat_axis=0, tiled=True)
        from_y = [
            lax.ppermute(by_y[k], "y", [(at, at ^ k) for at in range(down_across[0])])
            for k in range(1, down_across[0])
        ]
        from_x, *from_y = lax.optimization_barrier((from_x, *from_y))
        total = sum((part.astype(f32) for part in from_y), by_y[0].astype(f32))
        return jnp.sum(from_x.astype(f32), axis=0).astype(bf16), total.astype(bf16)

    last_first, last_second = sum_both(*last_lines)
    last_second, last_first = sum_both(last_second, last_first)
    last_parts = [last_first, last_second]

    grad_attn_input = keep.astype(f32) + swap(give, "core").astype(f32)
    grad_attn_input = scatter_sum(grad_attn_input, "zl", 0)
    norm_one, inv_one = layer_norm(x_mine.astype(f32))
    scaled = grad_attn_input * (1.0 + mod_mine[1:2])
    input_grad = grad_attn_mine + inv_one * (
        scaled
        - jnp.mean(scaled, axis=-1, keepdims=True)
        - norm_one * jnp.mean(scaled * norm_one, axis=-1, keepdims=True)
    )
    mlp_sum, input_grad, rest_sum, *last_parts = lax.optimization_barrier(
        (mlp_sum, input_grad, rest_sum, *last_parts)
    )
    up_lines = line_rows * (hidden // PACK)
    rest = jnp.concatenate(
        jnp.split(rest_sum, 5, 0) + last_parts + jnp.split(mlp_sum[:up_lines], hidden // PACK, 0), axis=1
    )
    lines = along_line(rest.reshape(8, rows_each, -1))
    up_rows = lines[..., -hidden:].reshape(8, rows_each, peers, hid_pad)[..., :hid_each]
    grad_mlp_in = jnp.transpose(up_rows, (1, 2, 0, 3)).reshape(rows_each, -1).astype(f32)
    down_rows = jnp.concatenate(jnp.split(mlp_sum[up_lines:], width // PACK, 0), axis=1)
    grad_mlp_out = down_rows[:hid_each].astype(f32)
    lines = lines[..., :-hidden].astype(f32).reshape(2, 2, 2, rows_each, -1)
    sides = lines[0, :, 0] + lines[0, :, 1] + lines[1, :, 0] + lines[1, :, 1]
    qkv_lines = (lines[0] + lines[1]).reshape(4, rows_each, -1)[..., 5 * REST : 5 * REST + 3 * local]
    grad_qkv_rows = jnp.transpose(qkv_lines.reshape(4, rows_each, 3, local), (1, 2, 0, 3))
    grad_qkv_rows = grad_qkv_rows.reshape(rows_each, -1)
    small_sum = (sides[0] + sides[1])[:, 5 * REST + 3 * local : 5 * REST + 3 * local + 12].T

    def whole_of(first, count):
        return jnp.concatenate(
            [
                sides[side, :, at * REST : (at + 1) * REST]
                for at in range(first, first + count)
                for side in range(2)
            ],
            axis=1,
        )

    return (
        result[None],
        input_grad[None],
        grad_qkv_rows, whole_of(0, 1), whole_of(1, 1), whole_of(2, 2), whole_of(4, 1),
        grad_mlp_in, grad_mlp_out,
        small_sum[0], small_sum[1], small_sum[2], small_sum[3], small_sum[4], small_sum[5],
        small_sum[6:],
    )


def solution(mesh):
    places = mesh.devices.size // 8
    across = min(places, 4)
    lines = Mesh(
        mesh.devices.reshape(places // across, across, 2, 2, 2), ("y", "x", "zh", "core", "zl")
    )
    clip = ("y", "x", "zh", "core")
    every = (*clip, "zl")
    tokens = P(clip, "zl", None)
    rows = P(every, None)
    return jax.shard_map(
        on_device,
        mesh=lines,
        in_specs=(tokens, P(clip, None, None), tokens, P(clip, None, "zl"))
        + (rows,) * 7 + (P(every),) * 6 + (P(None, every), tokens),
        out_specs=(tokens, tokens) + (rows,) * 7 + (P(every),) * 6 + (P(None, every),),
        check_vma=False,
    )
```

```python
import functools

import jax
import jax.numpy as jnp
from jax import lax
from jax.experimental import pallas as pl
from jax.experimental.pallas import tpu as pltpu
from jax.sharding import Mesh
from jax.sharding import PartitionSpec as P

HEADS = 12
HEAD_DIM = 128
NORM_EPS = 1e-06
SCALE = HEAD_DIM ** (-0.5)

bf16 = jnp.bfloat16
f32 = jnp.float32

GROUP = ("core", "zl")
CHIPS = ("zh", "zl")
LINE = ("zh", "core", "zl")
PLACES = ("y", "x")
SWAP = [(0, 1), (1, 0)]
CROSS = [(0, 3), (3, 0), (1, 2), (2, 1)]


def mm(left, right):
    return jnp.dot(left, right, preferred_element_type=f32)


def mm_tn(left, right):
    return lax.dot_general(left, right, (((0,), (0,)), ((), ())), preferred_element_type=f32)


def mm_nt(left, right):
    return lax.dot_general(left, right, (((1,), (1,)), ((), ())), preferred_element_type=f32)


def swap(array, axis_name):
    return lax.ppermute(array, axis_name, SWAP)


def others(array, axis_name):
    size = lax.axis_size(axis_name)
    return [array] + [
        lax.ppermute(array, axis_name, [(i, i ^ k) for i in range(size)]) for k in range(1, size)
    ]


def in_order(parts, index):
    step = 1
    parts = list(parts)
    while step < len(parts):
        turned = index // step % 2 == 1
        for k in range(len(parts)):
            if k & step == 0:
                low, high = parts[k], parts[k + step]
                parts[k], parts[k + step] = jnp.where(turned, high, low), jnp.where(turned, low, high)
        step *= 2
    return parts


def axis_join(piece, axis_name, dim=0):
    return jnp.concatenate(in_order(others(piece, axis_name), lax.axis_index(axis_name)), dim)


def group_sum(small):
    return (
        small + swap(small, "zl") + swap(small, "core") + lax.ppermute(small, GROUP, CROSS)
    )


def core_sum(small):
    return small + swap(small, "core")


def ordered(mine, other, axis_name, dim):
    first = lax.axis_index(axis_name) == 0
    return jnp.where(
        first, jnp.concatenate([mine, other], dim), jnp.concatenate([other, mine], dim)
    )


def join(piece, axis_name, dim):
    return ordered(piece, swap(piece, axis_name), axis_name, dim)


def halves(whole, axis_name, dim):
    low, high = jnp.split(whole, 2, dim)
    first = lax.axis_index(axis_name) == 0
    return jnp.where(first, low, high), jnp.where(first, high, low)


def trade(whole, axis_name, cut, lay):
    keep, give = halves(whole, axis_name, cut)
    return ordered(keep, swap(give, axis_name), axis_name, lay)


def scatter_sum(partial, axis_name, dim):
    keep, give = halves(partial, axis_name, dim)
    return keep.astype(f32) + swap(give.astype(bf16), axis_name).astype(f32)


def by_seq(rows):
    return rows.reshape(2, rows.shape[0] // 2, rows.shape[1])


def flat(rows):
    return rows.reshape(-1, rows.shape[-1])


def layer_norm(values):
    centred = values - jnp.mean(values, axis=-1, keepdims=True)
    inv = lax.rsqrt(jnp.mean(centred * centred, axis=-1, keepdims=True) + NORM_EPS)
    return centred * inv, inv


def split_norm(values):
    local = values.shape[1]
    mean_here = jnp.mean(values, axis=-1)
    centred = values - mean_here[:, None]
    mine = jnp.stack([mean_here, jnp.sum(centred * centred, axis=-1)])
    other = swap(mine, "core")
    mean = (mine[0] + other[0]) / 2
    apart = mine[0] - mean
    spread = mine[1] + other[1] + 2 * local * apart * apart
    inv = lax.rsqrt(spread / (2 * local) + NORM_EPS)
    return (values - mean[:, None]) * inv[:, None], inv


def turn(values, cos, sin):
    lanes = lax.broadcasted_iota(jnp.int32, values.shape, 1)
    swapped = jnp.where(
        lanes % 2 == 0,
        -pltpu.roll(values, HEAD_DIM - 1, 1),
        pltpu.roll(values, 1, 1),
    )
    return values * cos + swapped * sin


def attend(query, key):
    scores = mm_nt(query, key) * SCALE
    peak = jnp.max(scores, axis=-1, keepdims=True)
    weights = jnp.exp(scores - peak)
    weights = weights / jnp.sum(weights, axis=-1, keepdims=True)
    return weights


def attend_grads(query, key, value, grad):
    weights = attend(query, key)
    grad_weights = mm_nt(grad, value)
    delta = jnp.sum(weights * grad_weights, axis=-1, keepdims=True)
    grad_scores = (weights * (grad_weights - delta)).astype(bf16)
    grad_query = mm(grad_scores, key) * SCALE
    grad_key = mm_tn(grad_scores, query) * SCALE
    grad_value = mm_tn(weights.astype(bf16), grad)
    return grad_query, grad_key, grad_value


def self_forward_kernel(q_ref, k_ref, v_ref, r_ref, gq_ref, gk_ref, cos_ref, sin_ref,
                        qr_ref, kr_ref, vb_ref, o_ref):
    cos, sin = cos_ref[...], sin_ref[...]
    query = turn(q_ref[...] * r_ref[:, 0:1] * gq_ref[...], cos, sin).astype(bf16)
    key = turn(k_ref[...] * r_ref[:, 1:2] * gk_ref[...], cos, sin).astype(bf16)
    value = v_ref[...].astype(bf16)
    qr_ref[...] = query
    kr_ref[...] = key
    vb_ref[...] = value
    weights = attend(query, key).astype(bf16)
    o_ref[...] = mm(weights, value).astype(bf16)


def self_forward(qkv, inverse, gain_q, gain_k, cos, sin, clips):
    rows, local = qkv.shape[0], qkv.shape[1] // 3
    heads, tokens = local // HEAD_DIM, rows // clips

    def at(shift):
        return pl.BlockSpec((tokens, HEAD_DIM), lambda b, h, s=shift: (b, h + s))

    gain = pl.BlockSpec((1, HEAD_DIM), lambda b, h: (0, h))
    table = pl.BlockSpec((tokens, HEAD_DIM), lambda b, h: (b, 0))
    return pl.pallas_call(
        self_forward_kernel,
        grid=(clips, heads),
        in_specs=[at(0), at(heads), at(2 * heads),
                  pl.BlockSpec((tokens, 2), lambda b, h: (b, 0)), gain, gain, table, table],
        out_specs=[at(0)] * 4,
        out_shape=[jax.ShapeDtypeStruct((rows, local), bf16)] * 4,
        cost_estimate=pl.CostEstimate(flops=8 * 10**9, bytes_accessed=10**7, transcendentals=10**6),
        name="self_forward",
    )(qkv, qkv, qkv, inverse, gain_q, gain_k, cos, sin)


def self_backward_kernel(qr_ref, kr_ref, vb_ref, do_ref, q_ref, k_ref, r_ref, gq_ref, gk_ref,
                         cos_ref, sin_ref, uq_ref, uk_ref, dv_ref, part_ref, dgain_ref):
    cos, sin = cos_ref[...], sin_ref[...]
    grad_query, grad_key, grad_value = attend_grads(
        qr_ref[...], kr_ref[...], vb_ref[...], do_ref[...]
    )
    up_q = turn(grad_query, cos, -sin)
    up_k = turn(grad_key, cos, -sin)
    dv_ref[...] = grad_value.astype(bf16)
    vq, vk = up_q * q_ref[...], up_k * k_ref[...]
    dgain_ref[0, 0, 0:1, :] = jnp.sum(vq * r_ref[:, 0:1], axis=0, keepdims=True)
    dgain_ref[0, 0, 1:2, :] = jnp.sum(vk * r_ref[:, 1:2], axis=0, keepdims=True)
    up_q, up_k = up_q * gq_ref[...], up_k * gk_ref[...]
    uq_ref[...] = up_q
    uk_ref[...] = up_k
    mean_q = jnp.sum(vq * gq_ref[...], axis=-1, keepdims=True)
    mean_k = jnp.sum(vk * gk_ref[...], axis=-1, keepdims=True)
    both = jnp.concatenate([mean_q, mean_k], axis=1)

    @pl.when(pl.program_id(1) == 0)
    def _():
        part_ref[...] = both

    @pl.when(pl.program_id(1) > 0)
    def _():
        part_ref[...] += both


def self_backward(qr, kr, vb, grad, qkv, inverse, gain_q, gain_k, cos, sin, clips):
    rows, local = qr.shape
    heads, tokens = local // HEAD_DIM, rows // clips

    def at(shift):
        return pl.BlockSpec((tokens, HEAD_DIM), lambda b, h, s=shift: (b, h + s))

    gain = pl.BlockSpec((1, HEAD_DIM), lambda b, h: (0, h))
    table = pl.BlockSpec((tokens, HEAD_DIM), lambda b, h: (b, 0))
    pair = pl.BlockSpec((tokens, 2), lambda b, h: (b, 0))
    return pl.pallas_call(
        self_backward_kernel,
        grid=(clips, heads),
        in_specs=[at(0)] * 4 + [at(0), at(heads), pair, gain, gain, table, table],
        out_specs=[at(0)] * 3 + [pair, pl.BlockSpec((1, 1, 2, HEAD_DIM), lambda b, h: (b, h, 0, 0))],
        out_shape=[
            jax.ShapeDtypeStruct((rows, local), f32),
            jax.ShapeDtypeStruct((rows, local), f32),
            jax.ShapeDtypeStruct((rows, local), bf16),
            jax.ShapeDtypeStruct((rows, 2), f32),
            jax.ShapeDtypeStruct((clips, heads, 2, HEAD_DIM), f32),
        ],
        cost_estimate=pl.CostEstimate(flops=11 * 10**9, bytes_accessed=10**7, transcendentals=10**6),
        name="self_backward",
    )(qr, kr, vb, grad, qkv, qkv, inverse, gain_q, gain_k, cos, sin)


def cross_forward_kernel(q_ref, r_ref, g_ref, k_ref, v_ref, qn_ref, o_ref):
    tokens, words = q_ref.shape[0] // 2, k_ref.shape[0] // 2
    for clip in range(2):
        rows, text = pl.ds(clip * tokens, tokens), pl.ds(clip * words, words)
        query = (q_ref[rows, :] * r_ref[rows, :] * g_ref[...]).astype(bf16)
        qn_ref[rows, :] = query
        weights = attend(query, k_ref[text, :]).astype(bf16)
        o_ref[rows, :] = mm(weights, v_ref[text, :]).astype(bf16)


def cross_forward(cq, inverse, gain, key, value):
    rows, local = cq.shape
    at = pl.BlockSpec((rows, HEAD_DIM), lambda h: (0, h))
    text = pl.BlockSpec((key.shape[0], HEAD_DIM), lambda h: (0, h))
    return pl.pallas_call(
        cross_forward_kernel,
        grid=(local // HEAD_DIM,),
        in_specs=[at, pl.BlockSpec((rows, 1), lambda h: (0, 0)),
                  pl.BlockSpec((1, HEAD_DIM), lambda h: (0, h)), text, text],
        out_specs=[at, at],
        out_shape=[jax.ShapeDtypeStruct((rows, local), bf16)] * 2,
        cost_estimate=pl.CostEstimate(flops=9 * 10**9, bytes_accessed=10**7, transcendentals=10**6),
        name="cross_forward",
    )(cq, inverse, gain, key, value)


def cross_backward_kernel(qn_ref, k_ref, v_ref, do_ref, dq_ref, dk_ref, dv_ref):
    tokens, words = qn_ref.shape[0] // 2, k_ref.shape[0] // 2
    for clip in range(2):
        rows, text = pl.ds(clip * tokens, tokens), pl.ds(clip * words, words)
        grad_query, grad_key, grad_value = attend_grads(
            qn_ref[rows, :], k_ref[text, :], v_ref[text, :], do_ref[rows, :]
        )
        dq_ref[rows, :] = grad_query
        dk_ref[text, :] = grad_key
        dv_ref[text, :] = grad_value.astype(bf16)


def cross_backward(query, key, value, grad):
    rows, local = query.shape
    at = pl.BlockSpec((rows, HEAD_DIM), lambda h: (0, h))
    text = pl.BlockSpec((key.shape[0], HEAD_DIM), lambda h: (0, h))
    return pl.pallas_call(
        cross_backward_kernel,
        grid=(local // HEAD_DIM,),
        in_specs=[at, text, text, at],
        out_specs=[at, text, text],
        out_shape=[
            jax.ShapeDtypeStruct((rows, local), f32),
            jax.ShapeDtypeStruct(key.shape, f32),
            jax.ShapeDtypeStruct(key.shape, bf16),
        ],
        cost_estimate=pl.CostEstimate(flops=11 * 10**9, bytes_accessed=10**7, transcendentals=10**6),
        name="cross_backward",
    )(query, key, value, grad)


PACK = 256
REST = 768
GELU_A = 0.7978845608028654
GELU_B = 0.044715


def mlp_kernel(core_ref, x_ref, xo_ref, g_ref, go_ref, pack_ref, act_ref, gh_ref, gx_ref, gxo_ref,
               up, down, act, gh, total, total_other, sems, out_sems):
    peers, up_rows, hidden = up.shape
    down_rows, width = down.shape[1:]
    half = width // 2
    cuts = [0, hidden // PACK // 2 * PACK, hidden]
    loads, last = [], 0
    for k in range(2):
        first, last = last, -(-cuts[k + 1] // down_rows)
        moves = [
            (pack_ref.at[:, pl.ds(at // PACK * up_rows, up_rows), :], up.at[:, :, pl.ds(at, PACK)])
            for at in range(cuts[k], cuts[k + 1], PACK)
        ]
        for at in range(0, width, PACK):
            line = hidden // PACK * up_rows + at // PACK * down_rows
            moves.append(
                (
                    pack_ref.at[pl.ds(first, last - first), pl.ds(line, down_rows), :],
                    down.at[pl.ds(first, last - first), :, pl.ds(at, PACK)],
                )
            )
        loads.append([pltpu.make_async_copy(*m, sems.at[k, i]) for i, m in enumerate(moves)])
        for copy in loads[-1]:
            copy.start()
    down_flat = down.reshape(peers * down_rows, width)
    up_flat = up.reshape(peers * up_rows, hidden)
    mine = pl.ds(pl.multiple_of(core_ref[0] * half, half), half)
    other = pl.ds(pl.multiple_of((1 - core_ref[0]) * half, half), half)
    stores = []
    for k in range(2):
        for copy in loads[k]:
            copy.wait()
        cols = pl.ds(cuts[k], cuts[k + 1] - cuts[k])
        pre = mm(x_ref[...], up_flat[mine, cols]) + mm(xo_ref[...], up_flat[other, cols])
        grad = mm_nt(g_ref[...], down_flat[cols, mine]) + mm_nt(go_ref[...], down_flat[cols, other])
        square = pre * pre
        tanh = jnp.tanh(GELU_A * pre * (1.0 + GELU_B * square))
        share = 0.5 * (1.0 + tanh)
        act[:, cols] = (pre * share).astype(bf16)
        slope = share + pre * (0.5 * GELU_A) * (1.0 - tanh * tanh) * (1.0 + 3 * GELU_B * square)
        grad = (grad * slope).astype(bf16)
        gh[:, cols] = grad
        for i, (here, there) in enumerate(((act, act_ref), (gh, gh_ref))):
            stores.append(pltpu.make_async_copy(here.at[:, cols], there.at[:, cols], out_sems.at[k, i]))
            stores[-1].start()
        for rows, sums, out in ((mine, total, gx_ref), (other, total_other, gxo_ref)):
            part = mm_nt(grad, up_flat[rows, cols])
            if k == 0:
                sums[...] = part
            else:
                out[...] = (sums[...] + part).astype(bf16)
    for copy in stores:
        copy.wait()


def mlp(core, inputs, grads, packed, up_rows, hidden, down_rows):
    rows, half = inputs[0].shape
    width = 2 * half
    peers = packed.shape[0]
    copies = -(-hidden // PACK // 2) + width // PACK
    vmem = pl.BlockSpec(memory_space=pltpu.VMEM)
    any_space = pl.BlockSpec(memory_space=pl.ANY)
    return pl.pallas_call(
        mlp_kernel,
        in_specs=[pl.BlockSpec(memory_space=pltpu.SMEM)] + [vmem] * 4 + [any_space],
        out_specs=[any_space, any_space, vmem, vmem],
        out_shape=[
            jax.ShapeDtypeStruct((rows, hidden), bf16),
            jax.ShapeDtypeStruct((rows, hidden), bf16),
            jax.ShapeDtypeStruct((rows, half), bf16),
            jax.ShapeDtypeStruct((rows, half), bf16),
        ],
        scratch_shapes=[
            pltpu.VMEM((peers, up_rows, hidden), bf16),
            pltpu.VMEM((peers, down_rows, width), bf16),
            pltpu.VMEM((rows, hidden), bf16),
            pltpu.VMEM((rows, hidden), bf16),
            pltpu.VMEM((rows, half), f32),
            pltpu.VMEM((rows, half), f32),
            pltpu.SemaphoreType.DMA((2, copies)),
            pltpu.SemaphoreType.DMA((2, 2)),
        ],
        compiler_params=pltpu.CompilerParams(vmem_limit_bytes=56 * 2**20),
        cost_estimate=pl.CostEstimate(
            flops=6 * rows * width * hidden, bytes_accessed=packed.size * 2, transcendentals=rows * hidden
        ),
        name="mlp",
    )(core, *inputs, *grads, packed)


def tn_pack_kernel(place, x_ref, g_ref, *rest):
    pack_ref, held, sems = rest[-3:]
    peers, rows, _ = held.shape[1:]
    slots = held.shape[0]
    copies = []
    for k in range(slots):
        grad = g_ref[:, k * REST : (k + 1) * REST]
        lines = held.at[k].reshape(peers * rows, REST)
        lines[...] = mm_tn(x_ref[...], grad).astype(bf16)
        copies.append(
            pltpu.make_async_copy(
                held.at[k], pack_ref.at[:, pl.ds((place + k) * rows, rows), :], sems.at[k]
            )
        )
        copies[-1].start()
    for copy in copies:
        copy.wait()


def tn_pack(left, right, place, places, peers, packed=None):
    width, slots = left.shape[1], right.shape[1] // REST
    rows = width // peers
    vmem = pl.BlockSpec(memory_space=pltpu.VMEM)
    any_space = pl.BlockSpec(memory_space=pl.ANY)
    given = [] if packed is None else [packed]
    return pl.pallas_call(
        functools.partial(tn_pack_kernel, place),
        in_specs=[vmem, vmem] + [any_space] * len(given),
        out_specs=any_space,
        out_shape=jax.ShapeDtypeStruct((peers, places * rows, REST), bf16),
        scratch_shapes=[pltpu.VMEM((slots, peers, rows, REST), bf16), pltpu.SemaphoreType.DMA((slots,))],
        input_output_aliases={2: 0} if given else {},
        compiler_params=pltpu.CompilerParams(vmem_limit_bytes=56 * 2**20),
        cost_estimate=pl.CostEstimate(
            flops=2 * left.size * right.shape[1], bytes_accessed=2 * width * right.shape[1], transcendentals=0
        ),
        name="tn_pack",
    )(left, right, *given)


def mlp_grads_kernel(core_ref, x_ref, xo_ref, gh_ref, act_ref, g_ref, go_ref, pack_ref, up, down, up_sems, down_sems):
    copies = []
    blocks, peers, rows, _ = up.shape
    some = peers // 2
    line = blocks * rows
    for part, left in enumerate((x_ref, xo_ref)):
        first = core_ref[0] if part == 0 else 1 - core_ref[0]
        grad = mm_tn(left[...], gh_ref[...]).astype(bf16)
        for k in range(blocks):
            held = up.at[k, pl.ds(part * some, some)]
            held[...] = grad[:, k * PACK : (k + 1) * PACK].reshape(some, rows, PACK)
            there = pack_ref.at[pl.ds(first * some, some), pl.ds(k * rows, rows), :]
            copies.append(pltpu.make_async_copy(held, there, up_sems.at[part, k]))
            copies[-1].start()
    blocks, _, rows, _ = down.shape
    for part, right in enumerate((g_ref, go_ref)):
        first = core_ref[0] if part == 0 else 1 - core_ref[0]
        grad = mm_tn(act_ref[...], right[...]).astype(bf16)
        for k in range(blocks // 2):
            held = down.at[part * (blocks // 2) + k]
            held[...] = grad[:, k * PACK : (k + 1) * PACK].reshape(peers, rows, PACK)
            at = pl.multiple_of(line + (first * (blocks // 2) + k) * rows, 16)
            there = pack_ref.at[:, pl.ds(at, rows), :]
            copies.append(pltpu.make_async_copy(held, there, down_sems.at[part, k]))
            copies[-1].start()
    for copy in copies:
        copy.wait()


def mlp_grads(core, inputs, grad_hidden, activated, grads, peers):
    width, hidden = 2 * inputs[0].shape[1], activated.shape[1]
    up_rows, down_rows = width // peers, hidden // peers
    lines = hidden // PACK * up_rows + width // PACK * down_rows
    vmem = pl.BlockSpec(memory_space=pltpu.VMEM)
    return pl.pallas_call(
        mlp_grads_kernel,
        in_specs=[pl.BlockSpec(memory_space=pltpu.SMEM)] + [vmem] * 6,
        out_specs=pl.BlockSpec(memory_space=pl.ANY),
        out_shape=jax.ShapeDtypeStruct((peers, lines, PACK), bf16),
        scratch_shapes=[
            pltpu.VMEM((hidden // PACK, peers, up_rows, PACK), bf16),
            pltpu.VMEM((width // PACK, peers, down_rows, PACK), bf16),
            pltpu.SemaphoreType.DMA((2, hidden // PACK)),
            pltpu.SemaphoreType.DMA((2, width // PACK // 2)),
        ],
        compiler_params=pltpu.CompilerParams(vmem_limit_bytes=56 * 2**20),
        cost_estimate=pl.CostEstimate(
            flops=4 * width * inputs[0].shape[0] * hidden, bytes_accessed=4 * width * hidden, transcendentals=0
        ),
        name="mlp_grads",
    )(core, *inputs, grad_hidden, activated, *grads)


def tail_kernel(places, at_ref, x_ref, g_ref, w_ref, n_ref, small_ref, first_ref, second_ref, keep_ref, give_ref, held):
    cut, some = first_ref.shape[1], x_ref.shape[0] // 2
    ones = jnp.ones((x_ref.shape[0], 128), bf16)
    part = mm_nt(g_ref[...], w_ref[...])
    low = part.astype(bf16)
    shift = mm_tn(low, ones)
    scale = mm_tn((part * n_ref[...].astype(f32)).astype(bf16), ones)
    lane = lax.broadcasted_iota(jnp.int32, shift.shape, 1)
    small = jnp.where(lane == 6, shift, jnp.where(lane == 7, scale, small_ref[...]))
    held[...] = small.astype(bf16)
    zero = at_ref[0] == 0
    keep_ref[...] = jnp.where(zero, low[:some], low[some:])
    give_ref[...] = jnp.where(zero, low[some:], low[:some])
    down, across = places
    lines = x_ref.shape[1] // (down * across)
    step = down * across // 2
    for k in range(2):
        rows = pl.ds(k * step * lines, step * lines)
        grad = mm_tn(x_ref[:, rows], g_ref[...]).astype(bf16)
        for i in range(step):
            y, x = divmod(k * step + i, across)
            y = y ^ at_ref[1]
            here = slice(i * lines, (i + 1) * lines)
            there = pl.ds(pl.multiple_of((x * down + y) * lines, 16), lines)
            first_ref[there, :] = grad[here, :cut]
            there = pl.ds(pl.multiple_of((y * across + x) * lines, 16), lines)
            second_ref[there, : g_ref.shape[1] - cut] = grad[here, cut:]
            second_ref[there, g_ref.shape[1] - cut :] = held[pl.ds((k * step + i) * lines, lines), :]


def tail(places, at, inputs, grad, weight, norm, small):
    rows, width = inputs.shape
    cut = (grad.shape[1] + 128) // 2
    out = [
        jax.ShapeDtypeStruct((width, cut), bf16),
        jax.ShapeDtypeStruct((width, cut), bf16),
        jax.ShapeDtypeStruct((rows // 2, width), bf16),
        jax.ShapeDtypeStruct((rows // 2, width), bf16),
    ]

    def first_block(shape):
        return pl.BlockSpec(shape, lambda i: (0, 0))

    return pl.pallas_call(
        functools.partial(tail_kernel, places),
        grid=(1,),
        in_specs=[pl.BlockSpec(memory_space=pltpu.SMEM)]
        + [first_block(s) for s in (inputs.shape, grad.shape, (width, grad.shape[1]), norm.shape, small.shape)],
        out_specs=[first_block(o.shape) for o in out],
        out_shape=out,
        scratch_shapes=[pltpu.VMEM((width, 128), bf16)],
        compiler_params=pltpu.CompilerParams(vmem_limit_bytes=56 * 2**20),
        cost_estimate=pl.CostEstimate(flops=8 * 10**9, bytes_accessed=10**7, transcendentals=0),
        name="tail",
    )(at, inputs, grad, weight, norm, small)


def inverse_freq(pair_total):
    return 1.0 / 10000.0 ** (jnp.arange(pair_total, dtype=f32) * 2.0 / (2.0 * pair_total))


def rotary_tables(places):
    pair_count = HEAD_DIM // 2
    side = pair_count // 3
    frame = pair_count - 2 * side
    freq = jnp.concatenate([inverse_freq(frame), inverse_freq(side), inverse_freq(side)])
    freq = jnp.repeat(freq, 2)[None, :]
    pair = lax.broadcasted_iota(jnp.int32, (1, HEAD_DIM), 1) // 2
    angles = jnp.where(
        pair < frame,
        places[0][:, None],
        jnp.where(pair < frame + side, places[1][:, None], places[2][:, None]),
    ) * freq
    return jnp.cos(angles), jnp.sin(angles)


def columns_for(weight, count, owners):
    rows = weight.shape[0]
    parts = jnp.transpose(weight.reshape(rows, count, owners, -1), (2, 0, 1, 3))
    return parts.reshape(owners, rows, -1)


def along_line(parts):
    return lax.all_to_all(parts, LINE, split_axis=0, concat_axis=0, tiled=True)


def for_line(group_parts=None, core_parts=None):
    if core_parts is not None:
        group_parts = jnp.repeat(core_parts, 2, axis=0)
    return jnp.concatenate([group_parts, group_parts], 0)


def first_then(first, *then):
    return lax.optimization_barrier((first, *then))[1:]


def on_device(
    latent_tokens, time_embed, text_tokens, positions,
    w_qkv, attn_out, cross_q, cross_kv, cross_out, mlp_in, mlp_out,
    gain_q, gain_k, gain_cq, gain_ck, norm_weight, norm_bias, modulation, cotangent,
):
    peers = lax.axis_size(PLACES)
    core, zl = lax.axis_index("core"), lax.axis_index("zl")
    width = latent_tokens.shape[2]
    half, local = width // 2, width // 4
    clips = 2
    rows_each = w_qkv.shape[0]
    line_rows = 8 * rows_each
    hid_each = mlp_out.shape[0]
    hid_pad = -(-hid_each * peers // 256) * 256 // peers
    hidden = peers * hid_pad

    x_mine = latent_tokens[0]
    x_wide = join(join(x_mine, "zl", 0), "core", 0)
    text = join(join(text_tokens[0], "zl", 0), "core", 0)
    small = jnp.concatenate(
        [v[None] for v in (gain_q, gain_k, gain_cq, gain_ck, norm_weight, norm_bias)] + [modulation], 0
    )
    small = jnp.pad(small.T, ((0, 0), (0, 116)))
    shard = along_line(
        jnp.concatenate(
            [
                for_line(group_parts=columns_for(w_qkv, 3, 4)),
                for_line(core_parts=columns_for(attn_out, 1, 2)),
                jnp.broadcast_to(small, (8, *small.shape)),
            ],
            axis=2,
        )
    ).reshape(line_rows, -1)
    first_weight = lax.all_gather(shard[:, : 3 * local + half], PLACES, axis=0, tiled=True)
    qkv_weight, out_weight = first_weight[:, : 3 * local], first_weight[:, 3 * local :]
    whole = shard[:, 3 * local + half : 3 * local + half + 12].T.reshape(1, -1)
    whole = axis_join(axis_join(whole, "x"), "y").reshape(peers, 12, line_rows)
    whole = jnp.transpose(whole, (1, 0, 2)).reshape(12, width).astype(f32)

    parts = jnp.concatenate(
        [columns_for(cross_q, 1, 2), columns_for(cross_kv, 2, 2), columns_for(cross_out, 1, 2)], axis=2
    )
    whole, parts = lax.optimization_barrier((whole, parts))
    cross_shard = along_line(for_line(core_parts=parts)).reshape(line_rows, -1)
    cross_weight = lax.all_gather(cross_shard, PLACES, axis=0, tiled=True)
    cq_weight = cross_weight[:, :half]
    ckv_weight = cross_weight[:, half : 3 * half]
    co_weight = cross_weight[:, 3 * half :]

    time_rows = join(time_embed, "core", 0)
    mod_wide = time_rows + whole[None, 6:]
    mod_mine = time_embed[0] + whole[6:]

    def here(rows, cut):
        picked = jnp.split(rows, 2, -1)
        rows = jnp.where(core == 0, picked[0], picked[1])
        if cut == 4:
            picked = jnp.split(rows, 2, -1)
            rows = jnp.where(zl == 0, picked[0], picked[1])
        return rows

    mod = here(mod_wide, 2)
    g_q, g_k = here(whole[0:1], 4), here(whole[1:2], 4)
    g_cq, g_ck, n_w, n_b = (here(whole[i : i + 1], 2) for i in range(2, 6))
    tokens = latent_tokens.shape[1]

    def per_clip(row):
        rows = mod[:, row]
        return jnp.broadcast_to(rows[:, None], (clips, tokens, half)).reshape(-1, half)

    places = join(join(positions[0].astype(f32), "zl", 1), "core", 1)
    cos, sin = rotary_tables(places)
    x_here = trade(x_mine, "core", 1, 0).astype(f32)
    up_here = trade(cotangent[0], "core", 1, 0).astype(f32)
    norm_wide, _ = layer_norm(x_wide.astype(f32))
    attn_input = norm_wide.reshape(clips, -1, width) * (1.0 + mod_wide[:, 1:2]) + mod_wide[:, 0:1]
    attn_input = flat(attn_input).astype(bf16)
    attn_input, text, x_here, up_here = lax.optimization_barrier((attn_input, text, x_here, up_here))

    qkv = mm(attn_input, qkv_weight)
    squares = jnp.sum((qkv * qkv).reshape(-1, 3, local)[:, :2], axis=-1).T
    inv_qk = lax.rsqrt(group_sum(squares) / width + NORM_EPS).T
    qr, kr, vb, heads = self_forward(qkv, inv_qk, g_q, g_k, cos, sin, clips)
    heads = flat(trade(heads.reshape(2, -1, local), "zl", 1, 2))
    attn_tokens = join(heads, "core", 1)

    up = mlp_in.reshape(rows_each, peers, 8, hid_each)
    up = jnp.pad(up, ((0, 0), (0, 0), (0, 0), (0, hid_pad - hid_each)))
    up = jnp.transpose(up, (2, 0, 1, 3)).reshape(8, rows_each, hidden)
    attn_tokens, up = lax.optimization_barrier((attn_tokens, up))
    up_shard = along_line(up).reshape(line_rows, hidden)
    down = jnp.pad(mlp_out, ((0, hid_pad - hid_each), (0, 0)))
    mlp_shard = jnp.concatenate(
        [up_shard[:, at : at + PACK] for at in range(0, hidden, PACK)]
        + [down[:, at : at + PACK] for at in range(0, width, PACK)],
        axis=0,
    )
    mlp_pack = lax.all_gather(mlp_shard, PLACES, axis=0)

    branch_one = mm(attn_tokens, out_weight)
    after_attn = x_here + branch_one * per_clip(2)
    norm_two, inv_two = split_norm(after_attn)
    cross_input = join((norm_two * n_w + n_b).astype(bf16), "core", 1)
    grad_three = (up_here * per_clip(5)).astype(bf16)
    cross_input, grad_three = lax.optimization_barrier((cross_input, grad_three))
    grad_three = others(grad_three, CHIPS)

    ckv = mm(text, ckv_weight)
    ck_pre = ckv[:, :half]
    inv_ck = lax.rsqrt(core_sum(jnp.sum(ck_pre * ck_pre, axis=-1)[None]) / width + NORM_EPS)[0]
    cross_key = (ck_pre * inv_ck[:, None] * g_ck).astype(bf16)
    cross_value = ckv[:, half:].astype(bf16)
    cq_pre = mm(cross_input, cq_weight)
    inv_cq = lax.rsqrt(core_sum(jnp.sum(cq_pre * cq_pre, axis=-1)[None]) / width + NORM_EPS)[0]
    cross_query, cross_heads = cross_forward(cq_pre, inv_cq[:, None], g_cq, cross_key, cross_value)
    cross_heads, *grad_three = lax.optimization_barrier((cross_heads, *grad_three))

    def both_cores(pieces):
        lines = jnp.concatenate(pieces, 0)
        return lines, swap(lines, "core")

    grad_three = both_cores(grad_three)
    cross_tokens = join(cross_heads, "core", 1)
    after_cross = after_attn + mm(cross_tokens, co_weight)

    norm_three, inv_three = split_norm(after_cross)
    mlp_input = (norm_three * (1.0 + per_clip(4)) + per_clip(3)).astype(bf16)
    mlp_input = both_cores(others(mlp_input, CHIPS))
    core_row = jnp.full((1,), core, jnp.int32)
    activated, grad_hidden, keep, give = mlp(
        core_row, mlp_input, grad_three, mlp_pack, line_rows, hidden, hid_pad
    )

    def to_near(blocks):
        return [lax.ppermute(blocks[k], CHIPS, [(i, i ^ (k + 1)) for i in range(4)]) for k in range(3)]

    def core_lines(keep, give):
        got = swap(give, "core")
        near = keep[: 2 * tokens].astype(f32) + got[: 2 * tokens].astype(f32)
        far = keep[2 * tokens :].astype(f32) + got[2 * tokens :].astype(f32)
        return near, jnp.split(far.astype(bf16), 3, 0)

    near_input, far = core_lines(keep, give)
    down_weight = jnp.concatenate(
        [
            mlp_pack[:, at : at + hid_pad].reshape(hidden, PACK)
            for at in range(line_rows * (hidden // PACK), mlp_pack.shape[1], hid_pad)
        ],
        axis=1,
    )
    near, three = core_lines(*halves(mm(activated, down_weight).astype(bf16), "core", 1))
    activated, grad_hidden, *far = lax.optimization_barrier((activated, grad_hidden, *far))
    far = to_near(far)
    mlp_lines = mlp_grads(core_row, mlp_input, grad_hidden, activated, grad_three, peers)
    mlp_lines, *far = lax.optimization_barrier((mlp_lines, *far))
    grad_mlp_input = near_input + sum(part.astype(f32) for part in far)
    mlp_lines = mlp_lines.reshape(-1, PACK)
    mlp_sum = lax.psum_scatter(mlp_lines, PLACES, scatter_dimension=0, tiled=True)

    def norm_back(grad, scaled, norm, inv):
        sums = core_sum(jnp.stack([jnp.sum(scaled, axis=-1), jnp.sum(scaled * norm, axis=-1)])) / width
        return (scaled - sums[0][:, None] - norm * sums[1][:, None]) * inv[:, None]

    grad_mod3 = jnp.sum(grad_mlp_input, axis=0)
    grad_mod4 = jnp.sum(grad_mlp_input * norm_three, axis=0)
    grad_cross = up_here + norm_back(
        grad_mlp_input, grad_mlp_input * (1.0 + per_clip(4)), norm_three, inv_three
    )
    grad_two = grad_cross.astype(bf16)

    grad_heads = scatter_sum(mm_nt(grad_two, co_weight).astype(bf16), "core", 1).astype(bf16)
    rest_lines = tn_pack(cross_tokens, grad_two, 4, 5, peers)
    grad_heads, near, *three = lax.optimization_barrier((grad_heads, near, *three))
    three = to_near(three)
    up_cq, up_ck, up_cv = cross_backward(cross_query, cross_key, cross_value, grad_heads)
    up_cq, *three = lax.optimization_barrier((up_cq, *three))
    branch_three = near + sum(part.astype(f32) for part in three)
    result_here = (after_cross + branch_three * per_clip(5)).astype(bf16)
    grad_mod5 = jnp.sum(up_here * branch_three, axis=0)
    result = trade(result_here, "core", 0, 1)

    def rms_back(grad, pre, inv, gain):
        mean = core_sum(jnp.sum(grad * pre * gain, axis=-1)[None])[0] / width
        gain_grad = jnp.sum(grad * pre * inv[:, None], axis=0)
        return (grad * gain - pre * (inv * inv * mean)[:, None]) * inv[:, None], gain_grad

    grad_cq, grad_gain_cq = rms_back(up_cq, cq_pre, inv_cq, g_cq)
    grad_cq = grad_cq.astype(bf16)
    grad_cross_input = scatter_sum(mm_nt(grad_cq, cq_weight).astype(bf16), "core", 1)
    grad_ck, grad_gain_ck = rms_back(up_ck, ck_pre, inv_ck, g_ck)
    grad_ckv = jnp.concatenate([grad_ck.astype(bf16), up_cv], axis=1)
    rest_lines = tn_pack(cross_input, grad_cq, 1, 5, peers, rest_lines)
    rest_lines = tn_pack(text, grad_ckv, 2, 5, peers, rest_lines)
    grad_n_w = jnp.sum(grad_cross_input * norm_two, axis=0)
    grad_n_b = jnp.sum(grad_cross_input, axis=0)
    grad_attn = grad_cross + norm_back(grad_cross_input, grad_cross_input * n_w, norm_two, inv_two)
    grad_attn_mine = trade(grad_attn, "core", 0, 1)

    grad_one = (grad_attn * per_clip(2)).astype(bf16)
    grad_mod2 = jnp.sum(grad_attn * branch_one, axis=0)
    grad_heads = scatter_sum(mm_nt(grad_one, out_weight).astype(bf16), "core", 1).astype(bf16)
    grad_heads = flat(trade(by_seq(grad_heads), "zl", 2, 1))
    rest_lines = tn_pack(attn_tokens, grad_one, 0, 5, peers, rest_lines)
    mlp_sum, rest_lines = lax.optimization_barrier((mlp_sum, rest_lines))
    rest_sum = lax.psum_scatter(rest_lines.reshape(-1, REST), PLACES, scatter_dimension=0, tiled=True)
    up_q, up_k, grad_v, part, dgain = self_backward(
        qr, kr, vb, grad_heads, qkv, inv_qk, g_q, g_k, cos, sin, clips
    )
    mean_qk = group_sum(part.T) / width
    pull = (mean_qk * (inv_qk * inv_qk).T).T
    grad_q = (up_q - qkv[:, :local] * pull[:, 0:1]) * inv_qk[:, 0:1]
    grad_k = (up_k - qkv[:, local : 2 * local] * pull[:, 1:2]) * inv_qk[:, 1:2]
    grad_qkv = jnp.concatenate([grad_q.astype(bf16), grad_k.astype(bf16), grad_v], axis=1)
    dgain = jnp.transpose(jnp.sum(dgain, axis=0), (1, 0, 2)).reshape(2, local)

    dgain = jnp.where(zl == 0, jnp.pad(dgain, ((0, 0), (0, local))), jnp.pad(dgain, ((0, 0), (local, 0))))
    halfs = jnp.concatenate(
        [
            dgain,
            jnp.stack(
                [
                    grad_gain_cq, grad_gain_ck, grad_n_w, grad_n_b,
                    jnp.zeros_like(grad_n_b), jnp.zeros_like(grad_n_b),
                    grad_mod2, grad_mod3, grad_mod4, grad_mod5,
                ]
            ),
        ],
        0,
    )
    smalls = jnp.where(
        core == 0, jnp.pad(halfs, ((0, 0), (0, half))), jnp.pad(halfs, ((0, 0), (half, 0)))
    )
    small_cols = jnp.pad(smalls.T, ((0, 0), (0, 116)))
    down_across = (lax.axis_size("y"), lax.axis_size("x"))
    at_row = jnp.stack([core, lax.axis_index("y")]).astype(jnp.int32)
    *last_lines, keep, give = tail(
        down_across, at_row, attn_input, grad_qkv, first_weight, norm_wide.astype(bf16), small_cols
    )

    def sum_both(by_x, by_y):
        by_x = by_x.reshape(down_across[1], -1, by_x.shape[-1])
        by_y = jnp.split(by_y, down_across[0], 0)
        from_x = lax.all_to_all(by_x, "x", split_axis=0, concat_axis=0, tiled=True)
        from_y = [
            lax.ppermute(by_y[k], "y", [(at, at ^ k) for at in range(down_across[0])])
            for k in range(1, down_across[0])
        ]
        from_x, *from_y = lax.optimization_barrier((from_x, *from_y))
        total = sum((part.astype(f32) for part in from_y), by_y[0].astype(f32))
        return jnp.sum(from_x.astype(f32), axis=0).astype(bf16), total.astype(bf16)

    last_first, last_second = sum_both(*last_lines)
    last_second, last_first = sum_both(last_second, last_first)
    last_parts = [last_first, last_second]

    grad_attn_input = keep.astype(f32) + swap(give, "core").astype(f32)
    grad_attn_input = scatter_sum(grad_attn_input, "zl", 0)
    norm_one, inv_one = layer_norm(x_mine.astype(f32))
    scaled = grad_attn_input * (1.0 + mod_mine[1:2])
    input_grad = grad_attn_mine + inv_one * (
        scaled
        - jnp.mean(scaled, axis=-1, keepdims=True)
        - norm_one * jnp.mean(scaled * norm_one, axis=-1, keepdims=True)
    )
    mlp_sum, input_grad, rest_sum, *last_parts = lax.optimization_barrier(
        (mlp_sum, input_grad, rest_sum, *last_parts)
    )
    up_lines = line_rows * (hidden // PACK)
    rest = jnp.concatenate(
        jnp.split(rest_sum, 5, 0) + last_parts + jnp.split(mlp_sum[:up_lines], hidden // PACK, 0), axis=1
    )
    lines = along_line(rest.reshape(8, rows_each, -1))
    up_rows = lines[..., -hidden:].reshape(8, rows_each, peers, hid_pad)[..., :hid_each]
    grad_mlp_in = jnp.transpose(up_rows, (1, 2, 0, 3)).reshape(rows_each, -1).astype(f32)
    down_rows = jnp.concatenate(jnp.split(mlp_sum[up_lines:], width // PACK, 0), axis=1)
    grad_mlp_out = down_rows[:hid_each].astype(f32)
    lines = lines[..., :-hidden].astype(f32).reshape(2, 2, 2, rows_each, -1)
    sides = lines[0, :, 0] + lines[0, :, 1] + lines[1, :, 0] + lines[1, :, 1]
    qkv_lines = (lines[0] + lines[1]).reshape(4, rows_each, -1)[..., 5 * REST : 5 * REST + 3 * local]
    grad_qkv_rows = jnp.transpose(qkv_lines.reshape(4, rows_each, 3, local), (1, 2, 0, 3))
    grad_qkv_rows = grad_qkv_rows.reshape(rows_each, -1)
    small_sum = (sides[0] + sides[1])[:, 5 * REST + 3 * local : 5 * REST + 3 * local + 12].T

    def whole_of(first, count):
        return jnp.concatenate(
            [
                sides[side, :, at * REST : (at + 1) * REST]
                for at in range(first, first + count)
                for side in range(2)
            ],
            axis=1,
        )

    return (
        result[None],
        input_grad[None],
        grad_qkv_rows, whole_of(0, 1), whole_of(1, 1), whole_of(2, 2), whole_of(4, 1),
        grad_mlp_in, grad_mlp_out,
        small_sum[0], small_sum[1], small_sum[2], small_sum[3], small_sum[4], small_sum[5],
        small_sum[6:],
    )


def solution(mesh):
    places = mesh.devices.size // 8
    across = min(places, 4)
    lines = Mesh(
        mesh.devices.reshape(places // across, across, 2, 2, 2), ("y", "x", "zh", "core", "zl")
    )
    clip = ("y", "x", "zh", "core")
    every = (*clip, "zl")
    tokens = P(clip, "zl", None)
    rows = P(every, None)
    return jax.shard_map(
        on_device,
        mesh=lines,
        in_specs=(tokens, P(clip, None, None), tokens, P(clip, None, "zl"))
        + (rows,) * 7 + (P(every),) * 6 + (P(None, every), tokens),
        out_specs=(tokens, tokens) + (rows,) * 7 + (P(every),) * 6 + (P(None, every),),
        check_vma=False,
    )
```
